128 devices in a mesh: row: 8 (over y_hi, x), col: 16 (over z, y_lo, core).
Axes of the slice: x: 4, y: 4 (y_hi: 2, y_lo: 2; y = y_hi * 2 + y_lo), z: 4, core: 2. Of those that a mesh axis runs over, the one named last changes fastest.
Arguments:
- acts: bfloat16 [2048, 8192], P('row', 'col'), may hold values from -6 to 6
- grads: bfloat16 [2048, 8192], P('col', 'row'), may hold values from -6 to 6
- basis_acts: bfloat16 [8192, 8192], P('col', 'row'), may hold values from -0.0625 to 0.0625
- basis_grads: bfloat16 [8192, 8192], P('row', 'col'), may hold values from -0.0625 to 0.0625
Outputs:
- correction: float32 [8192, 8192], P('col', 'row')
The draws below stay inside these ranges and needn't reach their ends.
All inputs are finite; a program needn't handle non-finite values.
Results may differ from the reference program's by a relative error of at most 0.0041.
Values may be sent and summed in bfloat16 or wider, within the bound.
A program may use at most 64 MiB of HBM per device.

```python
import jax
import jax.numpy as jnp

D = 8192
LEN = 1024
SEQS = 2
TOKENS = 2048


def level_of(rng, extent, pieces, least, top_value):
    level = 1.0
    for axis_at, shards_of in pieces:
        steps = jax.random.uniform(jax.random.fold_in(jax.random.fold_in(rng, 6), axis_at), (shards_of,), jnp.float32, least / len(pieces), top_value / len(pieces))
        level = level * jnp.repeat(jnp.exp(steps), extent[axis_at] // shards_of).reshape((-1,) + (1,) * (len(extent) - 1 - axis_at))
    return level


def bell_draw(rng, extent, scale, reach, pieces=(), kind=jnp.bfloat16):
    loudness = level_of(rng, extent, pieces, -0.22, 0.18) if pieces else 1.0
    result = jax.random.normal(rng, extent, jnp.float32) * scale * loudness
    return jnp.minimum(jnp.maximum(result, -reach), reach).astype(kind)


def setup_inputs(seed: int = 0) -> dict:
    keys = jax.random.split(jax.random.key(seed), 5)
    acts = bell_draw(keys[0], (TOKENS, D), 1.0, 6.0, ((0, 8), (1, 16)))
    grads = bell_draw(keys[1], (TOKENS, D), 1.0, 6.0, ((0, 16), (1, 8)))
    basis_acts = bell_draw(keys[2], (D, D), D ** -0.5, 0.0625, ((0, 16), (1, 8)))
    basis_grads = bell_draw(keys[3], (D, D), D ** -0.5, 0.0625, ((0, 8), (1, 16)))
    return dict(acts=acts, grads=grads, basis_acts=basis_acts, basis_grads=basis_grads)


def reference(acts, grads, basis_acts, basis_grads):
    rotated_acts = jnp.dot(acts, basis_acts, preferred_element_type=jnp.float32).astype(jnp.bfloat16)
    rotated_grads = jnp.dot(grads, basis_grads, preferred_element_type=jnp.float32).astype(jnp.bfloat16)
    total = jnp.zeros((D, D), jnp.float32)
    for seq in range(SEQS):
        grad_part = rotated_grads[seq * LEN:(seq + 1) * LEN]
        act_part = rotated_acts[seq * LEN:(seq + 1) * LEN]
        block = jnp.dot(grad_part.T, act_part, preferred_element_type=jnp.float32)
        total = total + block * block
    return total / (SEQS * LEN)
```

```python
import jax
import jax.numpy as jnp
from jax import lax
from jax.experimental import pallas as pl
from jax.experimental.pallas import tpu as pltpu
from jax.sharding import PartitionSpec as P

MESH = pl.DeviceIdType.MESH
F32, BF16 = jnp.float32, jnp.bfloat16

TOKENS, D, SEQS = 2048, 8192, 2
SHARDS = 8
HALF = TOKENS // SHARDS // 2
PIECE = HALF // SHARDS
WIDE = 1024
NARROW = WIDE // 2
GROUPS = 4
TILE = 256

UP = 2.0 ** 30


def encode(v):
    v = v * UP
    return (v * v * v).astype(BF16)


def decode(c):
    c = c.astype(F32)
    size = jnp.maximum(jnp.abs(c), 2.0 ** -126)
    return c * (jnp.exp2(jnp.log2(size) * (-2.0 / 3.0)) * (1.0 / UP))


class Chain:
    def __init__(self, **refs):
        self.__dict__.update(refs)
        self.copies = {}


def kernel(acts, grads, qa, qs, out,
           xa, xg, wa, wg, pa, pg, rot_a, rot_g, rot_ao, rot_go, gt,
           sp1a, sm1a, sp2a, sm2a, s3a, rp1a, rm1a, rp2a, rm2a, r3a,
           sp1g, sm1g, sp2g, sm2g, s3g, rp1g, rm1g, rp2g, rm2g, r3g,
           local_sem, send_sem, recv_sem):
    row, col = lax.axis_index("row"), lax.axis_index("col")
    yh, x = row // 4, row % 4
    z, yl, h = col // 4, (col // 2) % 2, col % 2

    def dev(yh, x, z, yl, h):
        return (yh * 4 + x, z * 4 + yl * 2 + h)

    x_plus, x_minus = dev(yh, (x + 1) % 4, z, yl, h), dev(yh, (x + 3) % 4, z, yl, h)
    z_plus, z_minus = dev(yh, x, (z + 1) % 4, yl, h), dev(yh, x, (z + 3) % 4, yl, h)
    y_far, y_near = dev(1 - yh, x, z, yl, h), dev(yh, x, z, 1 - yl, h)
    other = dev(yh, x, z, yl, 1 - h)

    barrier = pltpu.get_barrier_semaphore()
    neighbours = (x_plus, x_minus, z_plus, z_minus, y_far, y_near, other)
    for n in neighbours:
        pl.semaphore_signal(barrier, inc=1, device_id=n, device_id_type=MESH)

    sems = [0]
    started = []

    def send(chain, name, src, dst, to):
        i = sems[0]
        sems[0] += 1
        copy = pltpu.make_async_remote_copy(
            src_ref=src, dst_ref=dst, send_sem=send_sem.at[i], recv_sem=recv_sem.at[i],
            device_id=to, device_id_type=MESH)
        copy.start()
        started.append(copy)
        chain.copies[name] = copy

    def arrived(chain, *names):
        for name in names:
            chain.copies[name].wait_recv()

    def piece(q):
        return pl.ds(pl.multiple_of(q * PIECE, PIECE), PIECE)

    a = Chain(plus=x_plus, minus=x_minus, partner=y_far, sum_plus=z_plus, sum_minus=z_minus, sum_partner=y_near,
              q=lambda d, e: ((z + d) % 4) * 2 + (yl + e) % 2,
              x=xa, w=wa, p=pa, rot=rot_a, sp1=sp1a, sm1=sm1a, sp2=sp2a, sm2=sm2a, s3=s3a,
              rp1=rp1a, rm1=rm1a, rp2=rp2a, rm2=rm2a, r3=r3a)
    g = Chain(plus=z_plus, minus=z_minus, partner=y_near, sum_plus=x_plus, sum_minus=x_minus, sum_partner=y_far,
              q=lambda d, e: ((yh + e) % 2) * 4 + (x + d) % 4,
              x=xg, w=wg, p=pg, rot=rot_g, sp1=sp1g, sm1=sm1g, sp2=sp2g, sm2=sm2g, s3=s3g,
              rp1=rp1g, rm1=rm1g, rp2=rp2g, rm2=rm2g, r3=r3g)
    chains = (g, a)
    lo, hi = pl.ds(0, NARROW), pl.ds(NARROW, NARROW)
    mine = pl.ds(pl.multiple_of(h * HALF, HALF), HALF)
    its = pl.ds(pl.multiple_of((1 - h) * HALF, HALF), HALF)

    local = [
        pltpu.make_async_copy(grads, xg.at[0], local_sem.at[0]),
        pltpu.make_async_copy(acts.at[mine], xa.at[0, :, lo], local_sem.at[1]),
        pltpu.make_async_copy(qs, wg.at[:, lo], local_sem.at[2]),
        pltpu.make_async_copy(qa, wa.at[lo], local_sem.at[3]),
    ]
    for copy in local:
        copy.start()

    pl.semaphore_wait(barrier, len(neighbours))

    send(a, "swap", acts.at[its], xa.at[0, :, hi], other)
    send(g, "own+", grads, xg.at[3], z_plus)
    send(g, "own-", grads, xg.at[1], z_minus)
    send(g, "ownp", grads, xg.at[4], y_near)
    send(a, "own+lo", acts.at[mine], xa.at[3, :, lo], x_plus)
    send(a, "own-lo", acts.at[mine], xa.at[1, :, lo], x_minus)
    send(a, "ownplo", acts.at[mine], xa.at[4, :, lo], y_far)
    arrived(a, "swap")
    send(a, "own+hi", xa.at[0, :, hi], xa.at[3, :, hi], x_plus)
    send(a, "own-hi", xa.at[0, :, hi], xa.at[1, :, hi], x_minus)
    send(a, "ownphi", xa.at[0, :, hi], xa.at[4, :, hi], y_far)
    send(g, "w", qs, wg.at[:, hi], other)
    send(a, "w", qa, wa.at[hi], other)

    def forward_own(c):
        if c is a:
            arrived(c, "own+lo", "own+hi")
        else:
            arrived(c, "own+")
        send(c, "fwd+", c.x.at[3, :, lo], c.x.at[2, :, lo], c.plus)
        if c is a:
            arrived(c, "own-lo", "own-hi")
        else:
            arrived(c, "own-")
        send(c, "fwd-", c.x.at[1, :, hi], c.x.at[2, :, hi], c.minus)

    def send_partner(c):
        if c is a:
            arrived(c, "ownplo", "ownphi")
        else:
            arrived(c, "ownp")
        send(c, "p+lo", c.x.at[4, :, lo], c.x.at[7, :, lo], c.plus)
        send(c, "p-hi", c.x.at[4, :, hi], c.x.at[5, :, hi], c.minus)
        send(c, "p+hi", c.x.at[4, :, hi], c.x.at[7, :, hi], c.plus)
        send(c, "p-lo", c.x.at[4, :, lo], c.x.at[5, :, lo], c.minus)

    def forward_partner(c):
        arrived(c, "p+lo")
        send(c, "pfwd+", c.x.at[7, :, lo], c.x.at[6, :, lo], c.plus)
        arrived(c, "p-hi")
        send(c, "pfwd-", c.x.at[5, :, hi], c.x.at[6, :, hi], c.minus)
        arrived(c, "p+hi", "p-lo")

    def multiply(c, i):
        if i == 1:
            arrived(c, "fwd+", "fwd-")
        if i == 3:
            arrived(c, "pfwd+", "pfwd-")
        two = pl.ds(2 * i, 2)
        rows = c.x[two].reshape(2 * HALF, WIDE)

        @pl.loop(0, WIDE // TILE)
        def _(n):
            cols = pl.ds(pl.multiple_of(n * TILE, TILE), TILE)
            c.p[two, :, cols] = jnp.dot(rows, c.w[:, cols], preferred_element_type=F32).reshape(2, HALF, TILE)

    def first_sums(c, i):
        two = pl.ds(2 * i, 2)
        first, second = pl.ds(0, PIECE), pl.ds(PIECE, PIECE)
        c.sp1[i, :, first] = encode(c.p[two, piece(c.q(2, 0))])
        c.sp1[i, :, second] = encode(c.p[two, piece(c.q(1, 1))])
        send(c, f"1+{i}", c.sp1.at[i], c.rp1.at[i], c.sum_plus)
        c.sm1[i, :, first] = encode(c.p[two, piece(c.q(2, 1))])
        c.sm1[i, :, second] = encode(c.p[two, piece(c.q(3, 0))])
        send(c, f"1-{i}", c.sm1.at[i], c.rm1.at[i], c.sum_minus)

    def second_sums(c, i):
        two = pl.ds(2 * i, 2)
        first = pl.ds(0, PIECE)
        arrived(c, f"1+{i}")
        c.sp2[i] = encode(c.p[two, piece(c.q(1, 0))] + decode(c.rp1[i, :, first]))
        send(c, f"2+{i}", c.sp2.at[i], c.rp2.at[i], c.sum_plus)
        arrived(c, f"1-{i}")
        c.sm2[i] = encode(c.p[two, piece(c.q(3, 1))] + decode(c.rm1[i, :, first]))
        send(c, f"2-{i}", c.sm2.at[i], c.rm2.at[i], c.sum_minus)

    def third_sums(c, i):
        two = pl.ds(2 * i, 2)
        second = pl.ds(PIECE, PIECE)
        arrived(c, f"2+{i}", f"2-{i}")
        c.s3[i] = encode(c.p[two, piece(c.q(0, 1))] + decode(c.rp1[i, :, second]) + decode(c.rm2[i]))
        send(c, f"3{i}", c.s3.at[i], c.r3.at[i], c.sum_partner)
        own = piece(c.q(0, 0))
        c.p[two, own] = c.p[two, own] + decode(c.rm1[i, :, second]) + decode(c.rp2[i])

    def finish(c, i):
        two = pl.ds(2 * i, 2)
        own = piece(c.q(0, 0))
        arrived(c, f"3{i}")
        c.rot[two, own] = (c.p[two, own] + decode(c.r3[i])).astype(BF16)
        ref = c.rot.at[two, own]
        send(c, f"g+{i}", ref, ref, c.sum_plus)
        send(c, f"g-{i}", ref, ref, c.sum_minus)
        send(c, f"gp{i}", ref, ref, c.sum_partner)

    def spread(c, i):
        arrived(c, f"g+{i}", f"g-{i}")
        ref = c.rot.at[2 * i, piece(c.q(3, 0))]
        send(c, f"gf+{i}", ref, ref, c.sum_plus)
        ref = c.rot.at[2 * i + 1, piece(c.q(1, 0))]
        send(c, f"gf-{i}", ref, ref, c.sum_minus)
        arrived(c, f"gp{i}")
        ref = c.rot.at[pl.ds(2 * i, 2), piece(c.q(0, 1))]
        send(c, f"h+{i}", ref, ref, c.sum_plus)
        send(c, f"h-{i}", ref, ref, c.sum_minus)

    def spread_partner(c, i):
        arrived(c, f"h+{i}", f"h-{i}")
        ref = c.rot.at[2 * i, piece(c.q(3, 1))]
        send(c, f"hf+{i}", ref, ref, c.sum_plus)
        ref = c.rot.at[2 * i + 1, piece(c.q(1, 1))]
        send(c, f"hf-{i}", ref, ref, c.sum_minus)

    def share(c, i):
        two = pl.ds(2 * i, 2)
        arrived(c, f"gf+{i}", f"gf-{i}", f"hf+{i}", f"hf-{i}")
        if c is a:
            send(c, f"c{i}", rot_a.at[two], rot_ao.at[two], other)
        else:
            send(c, f"c{i}", rot_g.at[two, :, hi], rot_go.at[two], other)
            for j in (2 * i, 2 * i + 1):
                gt[j, :, pl.ds(0, HALF)] = rot_g[j, :, lo].T

    def settle(c, i):
        arrived(c, f"c{i}")
        if c is g:
            for j in (2 * i, 2 * i + 1):
                gt[j, :, pl.ds(HALF, HALF)] = rot_go[j].T

    for c in chains:
        forward_own(c)
    for c in chains:
        send_partner(c)
    for copy in local:
        copy.wait()
    for c in chains:
        arrived(c, "w")
        multiply(c, 0)
        first_sums(c, 0)
    for c in chains:
        multiply(c, 1)
        first_sums(c, 1)
    for c in chains:
        forward_partner(c)
    stages = (second_sums, third_sums, finish, spread, spread_partner, share, settle)
    for c in chains:
        second_sums(c, 0)
    for c in chains:
        multiply(c, 2)
        first_sums(c, 2)
    for c in chains:
        third_sums(c, 0)
        second_sums(c, 1)
    for c in chains:
        multiply(c, 3)
        first_sums(c, 3)
    for tick in range(len(stages) + GROUPS):
        for i in range(GROUPS):
            at = tick + 2 - i
            if i == 0 and tick == 0:
                at = 2
            if 0 <= at < len(stages) and not (i == 0 and at < 2) and not (i == 1 and at < 1):
                for c in chains:
                    stages[at](c, i)

    def a_slot(t):
        return (t % 4 + 4 - x) % 4 + 4 * ((t // 4 + yh) % 2)

    def g_slot(t):
        return (t // 2 + 4 - z) % 4 + 4 * ((t + yl) % 2)

    @pl.loop(0, WIDE // TILE)
    def _(n):
        cols = pl.ds(pl.multiple_of(n * TILE, TILE), TILE)
        total = None
        for seq in range(SEQS):
            block = None
            for t in range(seq * 4, seq * 4 + 4):
                rows = jnp.concatenate([rot_a[a_slot(t), :, cols], rot_ao[a_slot(t), :, cols]], axis=0)
                term = jnp.dot(gt[g_slot(t)], rows, preferred_element_type=F32)
                block = term if block is None else block + term
            total = block * block if total is None else total + block * block
        out[:, cols] = total * (1.0 / TOKENS)

    for copy in started:
        copy.wait_send()


def on_device(acts, grads, qa, qs):
    vm = pltpu.VMEM
    sums = [vm((GROUPS, 2, 2 * PIECE, WIDE), BF16)] * 2 + [vm((GROUPS, 2, PIECE, WIDE), BF16)] * 3
    return pl.pallas_call(
        kernel,
        out_shape=jax.ShapeDtypeStruct((NARROW, WIDE), F32),
        in_specs=[pl.BlockSpec(memory_space=pl.ANY)] * 4,
        out_specs=pl.BlockSpec(memory_space=pltpu.VMEM),
        scratch_shapes=[
            vm((SHARDS, HALF, WIDE), BF16), vm((SHARDS, HALF, WIDE), BF16),
            vm((WIDE, WIDE), BF16), vm((WIDE, WIDE), BF16),
            vm((SHARDS, HALF, WIDE), F32), vm((SHARDS, HALF, WIDE), F32),
            vm((SHARDS, HALF, WIDE), BF16), vm((SHARDS, HALF, WIDE), BF16),
            vm((SHARDS, HALF, WIDE), BF16), vm((SHARDS, HALF, NARROW), BF16),
            vm((SHARDS, NARROW, 2 * HALF), BF16),
            *sums, *sums, *sums, *sums,
            pltpu.SemaphoreType.DMA((4,)),
            pltpu.SemaphoreType.DMA((160,)), pltpu.SemaphoreType.DMA((160,)),
        ],
        compiler_params=pltpu.CompilerParams(
            collective_id=0, has_side_effects=True, vmem_limit_bytes=56 * 2 ** 20),
        cost_estimate=pl.CostEstimate(flops=6442450944, bytes_accessed=5 * 2 ** 20, transcendentals=0),
        name="rotate_and_correlate",
    )(acts, grads, qa, qs)


def solution(mesh):
    return jax.shard_map(
        on_device,
        mesh=mesh,
        in_specs=(P("row", "col"), P("col", "row"), P("col", "row"), P("row", "col")),
        out_specs=P("col", "row"),
        check_vma=False,
    )
```

```python
import jax
import jax.numpy as jnp
from jax import lax
from jax.experimental import pallas as pl
from jax.experimental.pallas import tpu as pltpu
from jax.sharding import PartitionSpec as P

MESH = pl.DeviceIdType.MESH
F32, BF16 = jnp.float32, jnp.bfloat16

TOKENS, D, SEQS = 2048, 8192, 2
SHARDS = 8
HALF = TOKENS // SHARDS // 2
PIECE = HALF // SHARDS
WIDE = 1024
NARROW = WIDE // 2
TILE = 256
COPIES = 288

UP = 2.0 ** 30

GROUPS = ((0, 1), (1, 1), (2, 1), (3, 1), (4, 1), (5, 1), (6, 1), (7, 1))

ORDER = (
    "gown", "aown", "gmm0", "amm0", "gplo", "gf-", "af+", "gf+", "af-", "gmm1", "gphi", "gmm2", "g2-0", "a2-0",
    "amm2", "amm1", "aplo", "gpf+", "amm3", "g2+0", "a2+0", "gmm4", "aphi", "g2-1", "g2+1", "amm4", "g2+2", "g2-2",
    "gmm3", "gmm5", "apf+", "g30", "gpf-", "gmm6", "a2+2", "a2-2", "g2-4", "g2+4", "a2+1", "a2-1", "gfin0", "a2-3",
    "apf-", "amm5", "g31", "amm6", "g32", "a2+3", "a2-4", "a30", "gh0", "g2+3", "g2-3", "a2+4", "gmm7", "a32",
    "gfin1", "g2-5", "g2+5", "gfin2", "a31", "afin0", "g2-6", "a2+5", "ggf-0", "afin2", "a2-5", "a2+6", "g2+6",
    "gh1", "a33", "g34", "a2-6", "a34", "afin1", "ggf+0", "gh2", "amm7", "ghf-0", "ghf+0", "ah0", "agf+0", "agf-0",
    "agf-2", "g33", "ah2", "a35", "agf+2", "afin3", "a36", "g2+7", "g2-7", "ggf+1", "ggf-1", "agf-1", "agf+1",
    "gfin4", "afin4", "g35", "ah1", "a2-7", "a2+7", "ggf+2", "ggf-2", "ahf+0", "ahf-0", "gfin3", "g36", "afin5",
    "ghf+1", "ah3", "ahf+2", "ghf-1", "ahf-2", "afin6", "ghf-2", "ghf+2", "agf+3", "agf-3", "gsh0", "gh4", "ah4",
    "g37", "agf-4", "gst0", "agf+4", "ahf-1", "ahf+1", "ggf-4", "ggf+4", "gfin5", "a37", "gh3", "ash0", "ggf-3",
    "ggf+3", "gsh1", "gfin6", "ah5", "agf+5", "agf-5", "gsh2", "ast0", "ahf+3", "ahf-3", "ah6", "gst1", "ghf+4",
    "ghf-4", "ash2", "gst2", "agf-6", "agf+6", "ggf-5", "ggf+5", "gfin7", "ast2", "ghf+3", "ghf-3", "gh5", "afin7",
    "ahf-4", "ahf+4", "ash1", "ggf-6", "ggf+6", "gh6", "gsh4", "ahf+5", "ahf-5", "ast1", "gh7", "ash3", "gst4",
    "ah7", "ggf+7", "ggf-7", "gsh3", "ahf-6", "ahf+6", "ast3", "ghf-5", "ghf+5", "gst3", "agf-7", "agf+7", "ash4",
    "ghf-6", "ghf+6", "ash5", "ghf+7", "ghf-7", "ahf+7", "ahf-7", "ast4", "ash6", "ast5", "gsh5", "gsh6", "ast6",
    "gst5", "gsh7", "ash7", "gst6", "gst7", "ast7",
)


def encode(v):
    v = v * UP
    return (v * v * v).astype(BF16)


def decode(c):
    c = c.astype(F32)
    size = jnp.maximum(jnp.abs(c), 2.0 ** -126)
    return c * (jnp.exp2(jnp.log2(size) * (-2.0 / 3.0)) * (1.0 / UP))


class Chain:
    def __init__(self, **refs):
        self.__dict__.update(refs)
        self.copies = {}


def kernel(acts, grads, qa, qs, out,
           xa, xg, wa, wg, pa, pg, rot_a, rot_g, rot_ao, rot_go, gt,
           sp1a, sm1a, sp2a, sm2a, s3a, rp1a, rm1a, rp2a, rm2a, r3a,
           sp1g, sm1g, sp2g, sm2g, s3g, rp1g, rm1g, rp2g, rm2g, r3g,
           local_sem, send_sem, recv_sem):
    row, col = lax.axis_index("row"), lax.axis_index("col")
    yh, x = row // 4, row % 4
    z, yl, h = col // 4, (col // 2) % 2, col % 2

    def dev(yh, x, z, yl, h):
        return (yh * 4 + x, z * 4 + yl * 2 + h)

    x_plus, x_minus = dev(yh, (x + 1) % 4, z, yl, h), dev(yh, (x + 3) % 4, z, yl, h)
    z_plus, z_minus = dev(yh, x, (z + 1) % 4, yl, h), dev(yh, x, (z + 3) % 4, yl, h)
    y_far, y_near = dev(1 - yh, x, z, yl, h), dev(yh, x, z, 1 - yl, h)
    other = dev(yh, x, z, yl, 1 - h)
    x_plus_o, x_minus_o = dev(yh, (x + 1) % 4, z, yl, 1 - h), dev(yh, (x + 3) % 4, z, yl, 1 - h)
    y_far_o = dev(1 - yh, x, z, yl, 1 - h)

    barrier = pltpu.get_barrier_semaphore()
    neighbours = (x_plus, x_minus, z_plus, z_minus, y_far, y_near, other, x_plus_o, x_minus_o, y_far_o)
    for n in neighbours:
        pl.semaphore_signal(barrier, inc=1, device_id=n, device_id_type=MESH)

    sems = [0]

    def send(chain, name, src, dst, to):
        i = sems[0]
        sems[0] += 1
        copy = pltpu.make_async_remote_copy(
            src_ref=src, dst_ref=dst, send_sem=send_sem.at[i], recv_sem=recv_sem.at[i],
            device_id=to, device_id_type=MESH)
        copy.start()
        chain.copies[name] = copy

    def arrived(chain, *names):
        for name in names:
            copy = chain.copies.pop(name, None)
            if copy is not None:
                copy.wait()

    def piece(q):
        return pl.ds(pl.multiple_of(q * PIECE, PIECE), PIECE)

    lo, hi = pl.ds(0, NARROW), pl.ds(NARROW, NARROW)
    mine = pl.ds(pl.multiple_of(h * HALF, HALF), HALF)
    its = pl.ds(pl.multiple_of((1 - h) * HALF, HALF), HALF)
    first, second = pl.ds(0, PIECE), pl.ds(PIECE, PIECE)

    a = Chain(plus=x_plus, minus=x_minus, partner=y_far, sum_plus=z_plus, sum_minus=z_minus, sum_partner=y_near,
              plus_o=x_plus_o, minus_o=x_minus_o, partner_o=y_far_o,
              own_lo=acts.at[mine], own_hi=acts.at[its],
              q=lambda d, e: ((z + d) % 4) * 2 + (yl + e) % 2,
              x=xa, w=wa, p=pa, rot=rot_a, sp1=sp1a, sm1=sm1a, sp2=sp2a, sm2=sm2a, s3=s3a,
              rp1=rp1a, rm1=rm1a, rp2=rp2a, rm2=rm2a, r3=r3a)
    g = Chain(plus=z_plus, minus=z_minus, partner=y_near, sum_plus=x_plus, sum_minus=x_minus, sum_partner=y_far,
              plus_o=z_plus, minus_o=z_minus, partner_o=y_near,
              own_lo=grads.at[:, lo], own_hi=grads.at[:, hi],
              q=lambda d, e: ((yh + e) % 2) * 4 + (x + d) % 4,
              x=xg, w=wg, p=pg, rot=rot_g, sp1=sp1g, sm1=sm1g, sp2=sp2g, sm2=sm2g, s3=s3g,
              rp1=rp1g, rm1=rm1g, rp2=rp2g, rm2=rm2g, r3=r3g)

    local = [
        pltpu.make_async_copy(grads, xg.at[0], local_sem.at[0]),
        pltpu.make_async_copy(acts.at[mine], xa.at[0, :, lo], local_sem.at[1]),
        pltpu.make_async_copy(qs, wg.at[:, lo], local_sem.at[2]),
        pltpu.make_async_copy(qa, wa.at[lo], local_sem.at[3]),
    ]
    for copy in local:
        copy.start()

    pl.semaphore_wait(barrier, len(neighbours))

    def own(c):
        send(c, "own+lo", c.own_lo, c.x.at[2, :, lo], c.plus)
        send(c, "own-hi", c.own_hi, c.x.at[1, :, hi], c.minus_o)
        send(c, "ownplo", c.own_lo, c.x.at[4, :, lo], c.partner)
        send(c, "own+hi", c.own_hi, c.x.at[2, :, hi], c.plus_o)
        send(c, "own-lo", c.own_lo, c.x.at[1, :, lo], c.minus)
        send(c, "ownphi", c.own_hi, c.x.at[4, :, hi], c.partner_o)
        if c is a:
            send(c, "swap", acts.at[its], xa.at[0, :, hi], other)
            send(c, "w", qa, wa.at[hi], other)
        else:
            send(c, "w", qs, wg.at[:, hi], other)

    def forward_plus(c):
        arrived(c, "own+lo")
        send(c, "fwd+", c.x.at[2, :, lo], c.x.at[3, :, lo], c.plus)

    def forward_minus(c):
        arrived(c, "own-hi")
        send(c, "fwd-", c.x.at[1, :, hi], c.x.at[3, :, hi], c.minus)

    def partner_lo(c):
        arrived(c, "ownplo")
        send(c, "p+lo", c.x.at[4, :, lo], c.x.at[6, :, lo], c.plus)
        send(c, "p-lo", c.x.at[4, :, lo], c.x.at[5, :, lo], c.minus)

    def partner_hi(c):
        arrived(c, "ownphi")
        send(c, "p-hi", c.x.at[4, :, hi], c.x.at[5, :, hi], c.minus)
        send(c, "p+hi", c.x.at[4, :, hi], c.x.at[6, :, hi], c.plus)

    def partner_forward_plus(c):
        arrived(c, "p+lo")
        send(c, "pfwd+", c.x.at[6, :, lo], c.x.at[7, :, lo], c.plus)

    def partner_forward_minus(c):
        arrived(c, "p-hi")
        send(c, "pfwd-", c.x.at[5, :, hi], c.x.at[7, :, hi], c.minus)

    needs = {0: ("swap",), 1: ("own-lo", "own-hi"), 2: ("own+lo", "own+hi"), 3: ("fwd+", "fwd-"),
             4: ("ownplo", "ownphi"), 5: ("p-lo", "p-hi"), 6: ("p+lo", "p+hi"), 7: ("pfwd+", "pfwd-")}

    def slots(j):
        return pl.ds(*GROUPS[j])

    def multiply(c, j):
        start, count = GROUPS[j]
        if j == 0:
            for copy in (local[0], local[2]) if c is g else (local[1], local[3]):
                copy.wait()
        arrived(c, "w")
        for slot in range(start, start + count):
            arrived(c, *needs[slot])

        @pl.loop(0, WIDE // TILE)
        def _(n):
            cols = pl.ds(pl.multiple_of(n * TILE, TILE), TILE)
            rows = c.x[slots(j)].reshape(count * HALF, WIDE)
            sums = jnp.dot(rows, c.w[:, cols], preferred_element_type=F32)
            c.p[slots(j), :, cols] = sums.reshape(count, HALF, TILE)

        c.sp1[slots(j), first] = encode(c.p[slots(j), piece(c.q(2, 0))])
        c.sp1[slots(j), second] = encode(c.p[slots(j), piece(c.q(1, 1))])
        send(c, f"1+{j}", c.sp1.at[slots(j)], c.rp1.at[slots(j)], c.sum_plus)
        c.sm1[slots(j), first] = encode(c.p[slots(j), piece(c.q(2, 1))])
        c.sm1[slots(j), second] = encode(c.p[slots(j), piece(c.q(3, 0))])
        send(c, f"1-{j}", c.sm1.at[slots(j)], c.rm1.at[slots(j)], c.sum_minus)

    def sum_plus(c, j):
        arrived(c, f"1+{j}")
        c.sp2[slots(j)] = encode(c.p[slots(j), piece(c.q(1, 0))] + decode(c.rp1[slots(j), first]))
        send(c, f"2+{j}", c.sp2.at[slots(j)], c.rp2.at[slots(j)], c.sum_plus)

    def sum_minus(c, j):
        arrived(c, f"1-{j}")
        c.sm2[slots(j)] = encode(c.p[slots(j), piece(c.q(3, 1))] + decode(c.rm1[slots(j), first]))
        send(c, f"2-{j}", c.sm2.at[slots(j)], c.rm2.at[slots(j)], c.sum_minus)

    def sum_partner(c, j):
        arrived(c, f"2+{j}", f"2-{j}")
        c.s3[slots(j)] = encode(c.p[slots(j), piece(c.q(0, 1))] + decode(c.rp1[slots(j), second]) + decode(c.rm2[slots(j)]))
        send(c, f"3{j}", c.s3.at[slots(j)], c.r3.at[slots(j)], c.sum_partner)
        at = piece(c.q(0, 0))
        c.p[slots(j), at] = c.p[slots(j), at] + decode(c.rm1[slots(j), second]) + decode(c.rp2[slots(j)])

    def finish(c, j):
        at = piece(c.q(0, 0))
        arrived(c, f"3{j}")
        c.rot[slots(j), at] = (c.p[slots(j), at] + decode(c.r3[slots(j)])).astype(BF16)
        ref = c.rot.at[slots(j), at]
        send(c, f"g+{j}", ref, ref, c.sum_plus)
        send(c, f"g-{j}", ref, ref, c.sum_minus)
        send(c, f"gp{j}", ref, ref, c.sum_partner)

    def spread_plus(c, j):
        arrived(c, f"g+{j}")
        ref = c.rot.at[slots(j), piece(c.q(3, 0)), lo]
        send(c, f"gf+{j}", ref, ref, c.sum_plus)

    def spread_minus(c, j):
        arrived(c, f"g-{j}")
        ref = c.rot.at[slots(j), piece(c.q(1, 0)), hi]
        send(c, f"gf-{j}", ref, ref, c.sum_minus)

    def spread_partner(c, j):
        arrived(c, f"gp{j}")
        ref = c.rot.at[slots(j), piece(c.q(0, 1))]
        send(c, f"h+{j}", ref, ref, c.sum_plus)
        send(c, f"h-{j}", ref, ref, c.sum_minus)

    def spread_partner_plus(c, j):
        arrived(c, f"h+{j}")
        ref = c.rot.at[slots(j), piece(c.q(3, 1)), lo]
        send(c, f"hf+{j}", ref, ref, c.sum_plus)

    def spread_partner_minus(c, j):
        arrived(c, f"h-{j}")
        ref = c.rot.at[slots(j), piece(c.q(1, 1)), hi]
        send(c, f"hf-{j}", ref, ref, c.sum_minus)

    def share(c, j):
        arrived(c, f"gf+{j}", f"gf-{j}", f"hf+{j}", f"hf-{j}")
        if c is a:
            send(c, f"c{j}", rot_a.at[slots(j)], rot_ao.at[slots(j)], other)
        else:
            send(c, f"c{j}", rot_g.at[slots(j), :, hi], rot_go.at[slots(j)], other)
            for slot in range(GROUPS[j][0], sum(GROUPS[j])):
                gt[slot, :, pl.ds(0, HALF)] = rot_g[slot, :, lo].T

    def settle(c, j):
        arrived(c, f"c{j}")
        if c is g:
            for slot in range(GROUPS[j][0], sum(GROUPS[j])):
                gt[slot, :, pl.ds(HALF, HALF)] = rot_go[slot].T

    whole = {"own": own, "f+": forward_plus, "f-": forward_minus, "plo": partner_lo, "phi": partner_hi,
             "pf+": partner_forward_plus, "pf-": partner_forward_minus}
    slotted = {"mm": multiply, "2+": sum_plus, "2-": sum_minus, "3": sum_partner, "fin": finish,
               "gf+": spread_plus, "gf-": spread_minus, "h": spread_partner,
               "hf+": spread_partner_plus, "hf-": spread_partner_minus, "sh": share, "st": settle}
    for step in ORDER:
        c = a if step[0] == "a" else g
        if step[1:] in whole:
            whole[step[1:]](c)
        else:
            slotted[step[1:-1]](c, int(step[-1]))
    for c in (a, g):
        arrived(c, *c.copies.copy())

    def ring_slot(up):
        return up + (up // 2) * (1 - 2 * (up % 2))

    def a_slot(t):
        return ring_slot((t % 4 + 4 - x) % 4) + 4 * ((t // 4 + yh) % 2)

    def g_slot(t):
        return ring_slot((t // 2 + 4 - z) % 4) + 4 * ((t + yl) % 2)

    @pl.loop(0, WIDE // TILE)
    def _(n):
        cols = pl.ds(pl.multiple_of(n * TILE, TILE), TILE)
        total = None
        for seq in range(SEQS):
            block = None
            for t in range(seq * 4, seq * 4 + 4):
                rows = jnp.concatenate([rot_a[a_slot(t), :, cols], rot_ao[a_slot(t), :, cols]], axis=0)
                term = jnp.dot(gt[g_slot(t)], rows, preferred_element_type=F32)
                block = term if block is None else block + term
            total = block * block if total is None else total + block * block
        out[:, cols] = total * (1.0 / TOKENS)


def on_device(acts, grads, qa, qs):
    vm = pltpu.VMEM
    sums = [vm((SHARDS, 2 * PIECE, WIDE), BF16)] * 2 + [vm((SHARDS, PIECE, WIDE), BF16)] * 3
    args = [pltpu.with_memory_space_constraint(v, pltpu.HBM) for v in (acts, grads, qa, qs)]
    return pl.pallas_call(
        kernel,
        out_shape=jax.ShapeDtypeStruct((NARROW, WIDE), F32),
        in_specs=[pl.BlockSpec(memory_space=pl.ANY)] * 4,
        out_specs=pl.BlockSpec(memory_space=pltpu.VMEM),
        scratch_shapes=[
            vm((SHARDS, HALF, WIDE), BF16), vm((SHARDS, HALF, WIDE), BF16),
            vm((WIDE, WIDE), BF16), vm((WIDE, WIDE), BF16),
            vm((SHARDS, HALF, WIDE), F32), vm((SHARDS, HALF, WIDE), F32),
            vm((SHARDS, HALF, WIDE), BF16), vm((SHARDS, HALF, WIDE), BF16),
            vm((SHARDS, HALF, WIDE), BF16), vm((SHARDS, HALF, NARROW), BF16),
            vm((SHARDS, NARROW, 2 * HALF), BF16),
            *sums, *sums, *sums, *sums,
            pltpu.SemaphoreType.DMA((4,)),
            pltpu.SemaphoreType.DMA((COPIES,)), pltpu.SemaphoreType.DMA((COPIES,)),
        ],
        compiler_params=pltpu.CompilerParams(
            collective_id=0, has_side_effects=True, vmem_limit_bytes=44 * 2 ** 20),
        cost_estimate=pl.CostEstimate(flops=6442450944, bytes_accessed=5 * 2 ** 20, transcendentals=0),
        name="rotate_and_correlate",
    )(*args)


def solution(mesh):
    return jax.shard_map(
        on_device,
        mesh=mesh,
        in_specs=(P("row", "col"), P("col", "row"), P("col", "row"), P("row", "col")),
        out_specs=P("col", "row"),
        check_vma=False,
    )
```

```python
import jax
import jax.numpy as jnp
from jax import lax
from jax.experimental import pallas as pl
from jax.experimental.pallas import tpu as pltpu
from jax.sharding import PartitionSpec as P

MESH = pl.DeviceIdType.MESH
F32, BF16 = jnp.float32, jnp.bfloat16

TOKENS, D, SEQS = 2048, 8192, 2
SLOTS = 8
HALF = TOKENS // SLOTS // 2
PIECE = HALF // SLOTS
WIDE = 1024
NARROW = WIDE // 2
TILE = 512
ARRIVALS = 160
SENT = 8000

UP = 2.0 ** 30

ORDER = (
    0, 1000, 70, 1070, 30, 20, 10, 1010, 1020, 40, 71, 1071, 72, 74, 1072, 80, 1030, 1080, 50, 1073, 1040, 81, 1074,
    73, 82, 84, 90, 76, 60, 75, 1081, 1082, 1050, 1090, 100, 1076, 1060, 1075, 1100, 91, 1083, 83, 120, 92, 77, 94,
    1091, 1084, 1120, 86, 1092, 101, 1086, 85, 102, 1085, 1101, 104, 1110, 1102, 1093, 110, 1077, 121, 1130, 93, 1094,
    122, 1121, 130, 1096, 1095, 1122, 87, 1111, 124, 1103, 96, 1112, 111, 103, 1104, 95, 1087, 1106, 112, 1140, 1105,
    114, 1131, 1123, 1150, 1132, 131, 132, 1113, 106, 140, 123, 1124, 97, 1114, 150, 134, 1097, 105, 1126, 1116, 113,
    1125, 1115, 1141, 141, 1133, 142, 126, 1142, 116, 1151, 151, 107, 1107, 152, 133, 1134, 1152, 144, 125, 115, 1136,
    154, 136, 1135, 1143, 117, 127, 1127, 143, 1117, 1144, 1153, 135, 1146, 153, 1145, 146, 1154, 160, 137, 1137,
    1156, 1155, 156, 145, 155, 161, 147, 1147, 157, 1157, 162,
)


def encode(v):
    v = v * UP
    return (v * v * v).astype(BF16)


def decode(c):
    c = c.astype(F32)
    size = jnp.maximum(jnp.abs(c), 2.0 ** -126)
    return c * (jnp.exp2(jnp.log2(size) * (-2.0 / 3.0)) * (1.0 / UP))


class Chain:
    def __init__(self, **refs):
        self.__dict__.update(refs)


def kernel(acts, grads, qa, qs, out, total,
           xa, xg, wa, wg, pa, pg, rot_a, rot_g, rot_ao, rot_go,
           s1a, r1a, s2a, r2a, s3a, r3a, s1g, r1g, s2g, r2g, s3g, r3g,
           local_sem, send_sem, recv_sem):
    row, col = lax.axis_index("row"), lax.axis_index("col")
    yh, x = row // 4, row % 4
    z, yl, h = col // 4, (col // 2) % 2, col % 2

    def dev(dyh, dx, dz, dyl, core):
        return ((yh + dyh) % 2 * 4 + (x + dx) % 4, (z + dz) % 4 * 4 + (yl + dyl) % 2 * 2 + core)

    x_plus, x_minus = dev(0, 1, 0, 0, h), dev(0, 3, 0, 0, h)
    z_plus, z_minus = dev(0, 0, 1, 0, h), dev(0, 0, 3, 0, h)
    y_far, y_near = dev(1, 0, 0, 0, h), dev(0, 0, 0, 1, h)
    other = dev(0, 0, 0, 0, 1 - h)
    x_plus_o, x_minus_o, y_far_o = dev(0, 1, 0, 0, 1 - h), dev(0, 3, 0, 0, 1 - h), dev(1, 0, 0, 0, 1 - h)

    barrier = pltpu.get_barrier_semaphore()
    neighbours = (x_plus, x_minus, z_plus, z_minus, y_far, y_near, other, x_plus_o, x_minus_o, y_far_o)
    for n in neighbours:
        pl.semaphore_signal(barrier, inc=1, device_id=n, device_id_type=MESH)

    names = {}

    def arrival(c, name):
        return recv_sem.at[names.setdefault((c.at,) + name, len(names))]

    def send(c, name, src, dst, to):
        pltpu.make_async_remote_copy(
            src_ref=src, dst_ref=dst, send_sem=send_sem, recv_sem=arrival(c, name),
            device_id=to, device_id_type=MESH).start()

    def arrived(c, name, ref):
        pltpu.make_async_remote_copy(
            src_ref=ref, dst_ref=ref, send_sem=send_sem, recv_sem=arrival(c, name),
            device_id=other, device_id_type=MESH).wait_recv()

    def piece(q):
        return pl.ds(pl.multiple_of(q * PIECE, PIECE), PIECE)

    lo, hi = pl.ds(0, NARROW), pl.ds(NARROW, NARROW)
    mine = pl.ds(pl.multiple_of(h * HALF, HALF), HALF)
    its = pl.ds(pl.multiple_of((1 - h) * HALF, HALF), HALF)
    first, second = pl.ds(0, PIECE), pl.ds(PIECE, PIECE)

    a = Chain(at=1, plus=x_plus, minus=x_minus, partner=y_far, sum_plus=z_plus, sum_minus=z_minus, sum_partner=y_near,
              plus_o=x_plus_o, minus_o=x_minus_o, partner_o=y_far_o,
              own_lo=acts.at[mine], own_hi=acts.at[its],
              q=lambda d, e: ((z + d) % 4) * 2 + (yl + e) % 2,
              x=xa, w=wa, p=pa, rot=rot_a, s1=s1a, r1=r1a, s2=s2a, r2=r2a, s3=s3a, r3=r3a)
    g = Chain(at=0, plus=z_plus, minus=z_minus, partner=y_near, sum_plus=x_plus, sum_minus=x_minus, sum_partner=y_far,
              plus_o=z_plus, minus_o=z_minus, partner_o=y_near,
              own_lo=grads.at[:, lo], own_hi=grads.at[:, hi],
              q=lambda d, e: ((yh + e) % 2) * 4 + (x + d) % 4,
              x=xg, w=wg, p=pg, rot=rot_g, s1=s1g, r1=r1g, s2=s2g, r2=r2g, s3=s3g, r3=r3g)

    local = [
        pltpu.make_async_copy(grads, xg.at[0], local_sem.at[0]),
        pltpu.make_async_copy(acts.at[mine], xa.at[0, :, lo], local_sem.at[1]),
        pltpu.make_async_copy(qs, wg.at[:, lo], local_sem.at[2]),
        pltpu.make_async_copy(qa, wa.at[lo], local_sem.at[3]),
    ]
    for copy in local:
        copy.start()

    pl.semaphore_wait(barrier, len(neighbours))

    UPWARD, DOWNWARD, SIDE = 0, 1, 2
    OWN, AHEAD, PARTNER, PARTNER_AHEAD, SWAP, BASIS, FIRST, SECOND, THIRD, DONE, ACROSS, HALVES, SHARED = range(13)

    def own(c):
        send(c, (OWN, UPWARD, 0), c.own_lo, c.x.at[2, :, lo], c.plus)
        send(c, (OWN, DOWNWARD, 1), c.own_hi, c.x.at[1, :, hi], c.minus_o)
        send(c, (OWN, SIDE, 0), c.own_lo, c.x.at[4, :, lo], c.partner)
        send(c, (OWN, UPWARD, 1), c.own_hi, c.x.at[2, :, hi], c.plus_o)
        send(c, (OWN, DOWNWARD, 0), c.own_lo, c.x.at[1, :, lo], c.minus)
        send(c, (OWN, SIDE, 1), c.own_hi, c.x.at[4, :, hi], c.partner_o)
        if c is a:
            send(c, (SWAP,), acts.at[its], xa.at[0, :, hi], other)
            send(c, (BASIS,), qa, wa.at[hi], other)
            out[...] = jnp.zeros_like(out)
        else:
            send(c, (BASIS,), qs, wg.at[:, hi], other)

    def forward_up(c):
        arrived(c, (OWN, UPWARD, 0), c.x.at[2, :, lo])
        send(c, (AHEAD,), c.x.at[2, :, lo], c.x.at[3, :, lo], c.plus)

    def forward_down(c):
        arrived(c, (OWN, DOWNWARD, 1), c.x.at[1, :, hi])
        send(c, (AHEAD,), c.x.at[1, :, hi], c.x.at[3, :, hi], c.minus)

    def partner_lo(c):
        arrived(c, (OWN, SIDE, 0), c.x.at[4, :, lo])
        send(c, (PARTNER, UPWARD, 0), c.x.at[4, :, lo], c.x.at[6, :, lo], c.plus)
        send(c, (PARTNER, DOWNWARD, 0), c.x.at[4, :, lo], c.x.at[5, :, lo], c.minus)

    def partner_hi(c):
        arrived(c, (OWN, SIDE, 1), c.x.at[4, :, hi])
        send(c, (PARTNER, DOWNWARD, 1), c.x.at[4, :, hi], c.x.at[5, :, hi], c.minus)
        send(c, (PARTNER, UPWARD, 1), c.x.at[4, :, hi], c.x.at[6, :, hi], c.plus)

    def partner_forward_up(c):
        arrived(c, (PARTNER, UPWARD, 0), c.x.at[6, :, lo])
        send(c, (PARTNER_AHEAD,), c.x.at[6, :, lo], c.x.at[7, :, lo], c.plus)

    def partner_forward_down(c):
        arrived(c, (PARTNER, DOWNWARD, 1), c.x.at[5, :, hi])
        send(c, (PARTNER_AHEAD,), c.x.at[5, :, hi], c.x.at[7, :, hi], c.minus)

    needs = {1: ((OWN, DOWNWARD, 0), lo), 2: ((OWN, UPWARD, 1), hi), 3: ((AHEAD,), None),
             5: ((PARTNER, DOWNWARD, 0), lo), 6: ((PARTNER, UPWARD, 1), hi), 7: ((PARTNER_AHEAD,), None)}
    begun = set()

    def multiply(c, j):
        if c.at not in begun:
            begun.add(c.at)
            for copy in (local[0], local[2]) if c is g else (local[1], local[3]):
                copy.wait()
            arrived(c, (BASIS,), c.w.at[hi])
        if j == 0 and c is a:
            arrived(c, (SWAP,), c.x.at[0, :, hi])
        if j in needs:
            name, cols = needs[j]
            arrived(c, name, c.x.at[j] if cols is None else c.x.at[j, :, cols])

        @pl.loop(0, WIDE // TILE)
        def _(n):
            cols = pl.ds(pl.multiple_of(n * TILE, TILE), TILE)
            c.p[j, :, cols] = jnp.dot(c.x[j], c.w[:, cols], preferred_element_type=F32)

        c.s1[j, UPWARD, first] = encode(c.p[j, piece(c.q(2, 0))])
        c.s1[j, UPWARD, second] = encode(c.p[j, piece(c.q(1, 1))])
        send(c, (FIRST, j), c.s1.at[j, UPWARD], c.r1.at[j, UPWARD], c.sum_plus)
        c.s1[j, DOWNWARD, first] = encode(c.p[j, piece(c.q(2, 1))])
        c.s1[j, DOWNWARD, second] = encode(c.p[j, piece(c.q(3, 0))])
        send(c, (FIRST, j), c.s1.at[j, DOWNWARD], c.r1.at[j, DOWNWARD], c.sum_minus)

    def sum_second(c, j):
        arrived(c, (FIRST, j), c.r1.at[j])
        c.s2[j, UPWARD] = encode(c.p[j, piece(c.q(1, 0))] + decode(c.r1[j, UPWARD, first]))
        send(c, (SECOND, j), c.s2.at[j, UPWARD], c.r2.at[j, UPWARD], c.sum_plus)
        c.s2[j, DOWNWARD] = encode(c.p[j, piece(c.q(3, 1))] + decode(c.r1[j, DOWNWARD, first]))
        send(c, (SECOND, j), c.s2.at[j, DOWNWARD], c.r2.at[j, DOWNWARD], c.sum_minus)

    def sum_partner(c, j):
        arrived(c, (SECOND, j), c.r2.at[j])
        c.s3[j] = encode(c.p[j, piece(c.q(0, 1))] + decode(c.r1[j, UPWARD, second]) + decode(c.r2[j, DOWNWARD]))
        send(c, (THIRD, j), c.s3.at[j], c.r3.at[j], c.sum_partner)
        at = piece(c.q(0, 0))
        c.p[j, at] = c.p[j, at] + decode(c.r1[j, DOWNWARD, second]) + decode(c.r2[j, UPWARD])

    def finish(c, j):
        at = piece(c.q(0, 0))
        arrived(c, (THIRD, j), c.r3.at[j])
        c.rot[j, at] = (c.p[j, at] + decode(c.r3[j])).astype(BF16)
        ref = c.rot.at[j, at]
        send(c, (DONE, j), ref, ref, c.sum_plus)
        send(c, (DONE, j), ref, ref, c.sum_minus)
        send(c, (DONE, SIDE, j), ref, ref, c.sum_partner)

    def spread(c, j):
        arrived(c, (DONE, j), c.rot.at[j, pl.ds(0, 2 * PIECE)])
        ref = c.rot.at[j, piece(c.q(3, 0)), lo]
        send(c, (HALVES, j), ref, ref, c.sum_plus)
        ref = c.rot.at[j, piece(c.q(1, 0)), hi]
        send(c, (HALVES, j), ref, ref, c.sum_minus)

    def across(c, j):
        arrived(c, (DONE, SIDE, j), c.rot.at[j, first])
        ref = c.rot.at[j, piece(c.q(0, 1))]
        send(c, (ACROSS, j), ref, ref, c.sum_plus)
        send(c, (ACROSS, j), ref, ref, c.sum_minus)

    def spread_across(c, j):
        arrived(c, (ACROSS, j), c.rot.at[j, pl.ds(0, 2 * PIECE)])
        ref = c.rot.at[j, piece(c.q(3, 1)), lo]
        send(c, (HALVES, j), ref, ref, c.sum_plus)
        ref = c.rot.at[j, piece(c.q(1, 1)), hi]
        send(c, (HALVES, j), ref, ref, c.sum_minus)

    def share(c, j):
        arrived(c, (HALVES, j), c.rot.at[j, pl.ds(0, 2 * PIECE)])
        if c is a:
            send(c, (SHARED, j), rot_a.at[j], rot_ao.at[j], other)
        else:
            send(c, (SHARED, j), rot_g.at[j, :, hi], rot_go.at[j], other)

    def receive(c, j):
        arrived(c, (SHARED, j), rot_ao.at[j] if c is a else rot_go.at[j])

    def ring_slot(up):
        return up + (up // 2) * (1 - 2 * (up % 2))

    def a_slot(t):
        return ring_slot((t % 4 + 4 - x) % 4) + 4 * ((t // 4 + yh) % 2)

    def g_slot(t):
        return ring_slot((t // 2 + 4 - z) % 4) + 4 * ((t + yl) % 2)

    def correlate(above, upto):
        @pl.loop(0, SLOTS)
        def _(t):
            last = jnp.maximum(a_slot(t), g_slot(t))

            @pl.when((last > above) & (last <= upto))
            def _():
                rows = jnp.concatenate([rot_g[g_slot(t), :, lo], rot_go[g_slot(t)]], axis=0)
                columns = jnp.concatenate([rot_a[a_slot(t)], rot_ao[a_slot(t)]], axis=0)
                out[t // 4] += lax.dot_general(
                    rows, columns, (((0,), (0,)), ((), ())), preferred_element_type=F32)

    steps = (own, forward_up, forward_down, partner_lo, partner_hi, partner_forward_up, partner_forward_down,
             multiply, sum_second, sum_partner, finish, spread, across, spread_across, share, receive)
    levels = (-1, 4, 6, 7)
    for code in ORDER:
        c, step, j = (g, a)[code // 1000], code % 1000 // 10, code % 10
        if step < 7:
            steps[step](c)
        elif step < len(steps):
            steps[step](c, j)
        else:
            correlate(levels[j], levels[j + 1])
    pltpu.make_async_copy(total, total, send_sem).wait()


def on_device(acts, grads, qa, qs):
    vm = pltpu.VMEM
    sums = [vm((SLOTS, 2, 2 * PIECE, WIDE), BF16)] * 2 + [vm((SLOTS, 2, PIECE, WIDE), BF16)] * 2
    sums += [vm((SLOTS, PIECE, WIDE), BF16)] * 2
    args = [pltpu.with_memory_space_constraint(v, pltpu.HBM) for v in (acts, grads, qa, qs)]
    blocks, _ = pl.pallas_call(
        kernel,
        out_shape=(jax.ShapeDtypeStruct((SEQS, NARROW, WIDE), F32), pltpu.HBM((SENT, WIDE), BF16)),
        in_specs=[pl.BlockSpec(memory_space=pl.ANY)] * 4,
        out_specs=(pl.BlockSpec(memory_space=pltpu.VMEM), pl.BlockSpec(memory_space=pltpu.HBM)),
        scratch_shapes=[
            vm((SLOTS, HALF, WIDE), BF16), vm((SLOTS, HALF, WIDE), BF16),
            vm((WIDE, WIDE), BF16), vm((WIDE, WIDE), BF16),
            vm((SLOTS, HALF, WIDE), F32), vm((SLOTS, HALF, WIDE), F32),
            vm((SLOTS, HALF, WIDE), BF16), vm((SLOTS, HALF, WIDE), BF16),
            vm((SLOTS, HALF, WIDE), BF16), vm((SLOTS, HALF, NARROW), BF16),
            *sums, *sums,
            pltpu.SemaphoreType.DMA((4,)),
            pltpu.SemaphoreType.DMA, pltpu.SemaphoreType.DMA((ARRIVALS,)),
        ],
        compiler_params=pltpu.CompilerParams(
            collective_id=0, has_side_effects=True, vmem_limit_bytes=44 * 2 ** 20),
        cost_estimate=pl.CostEstimate(flops=6442450944, bytes_accessed=5 * 2 ** 20, transcendentals=0),
        name="rotate_and_correlate",
    )(*args)
    return (blocks[0] * blocks[0] + blocks[1] * blocks[1]) * (1.0 / TOKENS)


def solution(mesh):
    return jax.shard_map(
        on_device,
        mesh=mesh,
        in_specs=(P("row", "col"), P("col", "row"), P("col", "row"), P("row", "col")),
        out_specs=P("col", "row"),
        check_vma=False,
    )
```

```python
import jax
import jax.numpy as jnp
from jax import lax
from jax.experimental import pallas as pl
from jax.experimental.pallas import tpu as pltpu
from jax.sharding import PartitionSpec as P

MESH = pl.DeviceIdType.MESH
F32, BF16 = jnp.float32, jnp.bfloat16

TOKENS, D, SEQS = 2048, 8192, 2
SLOTS = 8
HALF = TOKENS // SLOTS // 2
PIECE = HALF // SLOTS
WIDE = 1024
NARROW = WIDE // 2
TILE = 512
DIRECT = (6, 7)
ASIDE = (3,)
ARRIVALS = 160
SENT = 8000

UP = 2.0 ** 30

ORDER = (
    0, 1000, 70, 1070, 30, 20, 10, 1010, 1020, 40, 72, 1071, 71, 1072, 1080, 80, 74, 1030, 50, 1073, 1040, 82, 1074,
    73, 81, 90, 60, 75, 76, 1081, 1083, 84, 1050, 1082, 1090, 83, 100, 1060, 1075, 92, 1076, 1100, 91, 77, 85, 1091,
    1084, 120, 1093, 1092, 86, 102, 1120, 94, 1085, 1101, 101, 1086, 1102, 1110, 93, 1094, 122, 110, 1103, 1077, 1121,
    1130, 104, 87, 1095, 1122, 121, 95, 1111, 1104, 130, 1096, 96, 1112, 112, 1113, 1105, 124, 111, 103, 1087, 105,
    1124, 132, 1131, 1106, 1140, 114, 1132, 97, 106, 1150, 131, 1114, 140, 1123, 1125, 134, 150, 170, 1115, 1097, 113,
    1134, 1126, 125, 115, 1141, 142, 107, 1151, 152, 1142, 1143, 126, 1166, 141, 1107, 166, 144, 1135, 123, 1152,
    1144, 1153, 135, 151, 171, 172, 154, 1154, 1146, 127, 1127, 1156, 167, 1145, 143, 1167, 146, 145, 1155, 153, 174,
    173, 147, 155, 1147, 175, 156, 176, 1157, 157, 177,
)


def encode(v):
    v = v * UP
    return (v * v * v).astype(BF16)


def decode(c):
    c = c.astype(F32)
    size = jnp.maximum(jnp.abs(c), 2.0 ** -126)
    return c * (jnp.exp2(jnp.log2(size) * (-2.0 / 3.0)) * (1.0 / UP))


class Chain:
    def __init__(self, **refs):
        self.__dict__.update(refs)


def kernel(acts, grads, qa, qs, out, total,
           xa, xg, wa, wg, pa, pg, rot_a, rot_g, rot_ao, rot_go,
           s1a, r1a, s2a, r2a, s3a, r3a, s4a, r4a, s1g, r1g, s2g, r2g, s3g, r3g, s4g, r4g,
           local_sem, send_sem, recv_sem):
    row, col = lax.axis_index("row"), lax.axis_index("col")
    yh, x = row // 4, row % 4
    z, yl, h = col // 4, (col // 2) % 2, col % 2

    def dev(dyh, dx, dz, dyl, core):
        return ((yh + dyh) % 2 * 4 + (x + dx) % 4, (z + dz) % 4 * 4 + (yl + dyl) % 2 * 2 + core)

    x_plus, x_minus = dev(0, 1, 0, 0, h), dev(0, 3, 0, 0, h)
    z_plus, z_minus = dev(0, 0, 1, 0, h), dev(0, 0, 3, 0, h)
    y_far, y_near = dev(1, 0, 0, 0, h), dev(0, 0, 0, 1, h)
    other = dev(0, 0, 0, 0, 1 - h)
    x_plus_o, x_minus_o, y_far_o = dev(0, 1, 0, 0, 1 - h), dev(0, 3, 0, 0, 1 - h), dev(1, 0, 0, 0, 1 - h)

    barrier = pltpu.get_barrier_semaphore()
    x_two, z_two = dev(0, 2, 0, 0, h), dev(0, 0, 2, 0, h)
    neighbours = (x_plus, x_minus, z_plus, z_minus, y_far, y_near, other, x_plus_o, x_minus_o, y_far_o, x_two, z_two)
    for n in neighbours:
        pl.semaphore_signal(barrier, inc=1, device_id=n, device_id_type=MESH)

    names = {}

    def arrival(c, name):
        return recv_sem.at[names.setdefault((c.at,) + name, len(names))]

    def send(c, name, src, dst, to):
        pltpu.make_async_remote_copy(
            src_ref=src, dst_ref=dst, send_sem=send_sem, recv_sem=arrival(c, name),
            device_id=to, device_id_type=MESH).start()

    def arrived(c, name, ref):
        pltpu.make_async_remote_copy(
            src_ref=ref, dst_ref=ref, send_sem=send_sem, recv_sem=arrival(c, name),
            device_id=other, device_id_type=MESH).wait_recv()

    def piece(q):
        return pl.ds(pl.multiple_of(q * PIECE, PIECE), PIECE)

    lo, hi = pl.ds(0, NARROW), pl.ds(NARROW, NARROW)
    mine = pl.ds(pl.multiple_of(h * HALF, HALF), HALF)
    its = pl.ds(pl.multiple_of((1 - h) * HALF, HALF), HALF)
    first, second = pl.ds(0, PIECE), pl.ds(PIECE, PIECE)

    a = Chain(at=1, plus=x_plus, minus=x_minus, partner=y_far,
              sum_plus=z_plus, sum_minus=z_minus, sum_two=z_two, sum_partner=y_near,
              plus_o=x_plus_o, minus_o=x_minus_o, partner_o=y_far_o,
              own_lo=acts.at[mine], own_hi=acts.at[its],
              q=lambda d, e: ((z + d) % 4) * 2 + (yl + e) % 2,
              x=xa, w=wa, p=pa, rot=rot_a, s1=s1a, r1=r1a, s2=s2a, r2=r2a, s3=s3a, r3=r3a,
              s4=s4a, r4=r4a)
    g = Chain(at=0, plus=z_plus, minus=z_minus, partner=y_near,
              sum_plus=x_plus, sum_minus=x_minus, sum_two=x_two, sum_partner=y_far,
              plus_o=z_plus, minus_o=z_minus, partner_o=y_near,
              own_lo=grads.at[:, lo], own_hi=grads.at[:, hi],
              q=lambda d, e: ((yh + e) % 2) * 4 + (x + d) % 4,
              x=xg, w=wg, p=pg, rot=rot_g, s1=s1g, r1=r1g, s2=s2g, r2=r2g, s3=s3g, r3=r3g,
              s4=s4g, r4=r4g)

    local = [
        pltpu.make_async_copy(grads, xg.at[0], local_sem.at[0]),
        pltpu.make_async_copy(acts.at[mine], xa.at[0, :, lo], local_sem.at[1]),
        pltpu.make_async_copy(qs, wg.at[:, lo], local_sem.at[2]),
        pltpu.make_async_copy(qa, wa.at[lo], local_sem.at[3]),
    ]
    for copy in local:
        copy.start()

    pl.semaphore_wait(barrier, len(neighbours))

    UPWARD, DOWNWARD, SIDE = 0, 1, 2
    OWN, AHEAD, PARTNER, PARTNER_AHEAD, SWAP, BASIS, FIRST, SECOND, THIRD, DONE, ACROSS, HALVES, SHARED = range(13)

    def own(c):
        send(c, (OWN, UPWARD, 0), c.own_lo, c.x.at[2, :, lo], c.plus)
        send(c, (OWN, DOWNWARD, 1), c.own_hi, c.x.at[1, :, hi], c.minus_o)
        send(c, (OWN, SIDE, 0), c.own_lo, c.x.at[4, :, lo], c.partner)
        send(c, (OWN, UPWARD, 1), c.own_hi, c.x.at[2, :, hi], c.plus_o)
        send(c, (OWN, DOWNWARD, 0), c.own_lo, c.x.at[1, :, lo], c.minus)
        send(c, (OWN, SIDE, 1), c.own_hi, c.x.at[4, :, hi], c.partner_o)
        if c is a:
            send(c, (SWAP,), acts.at[its], xa.at[0, :, hi], other)
            send(c, (BASIS,), qa, wa.at[hi], other)
            out[...] = jnp.zeros_like(out)
        else:
            send(c, (BASIS,), qs, wg.at[:, hi], other)

    def forward_up(c):
        arrived(c, (OWN, UPWARD, 0), c.x.at[2, :, lo])
        send(c, (AHEAD,), c.x.at[2, :, lo], c.x.at[3, :, lo], c.plus)

    def forward_down(c):
        arrived(c, (OWN, DOWNWARD, 1), c.x.at[1, :, hi])
        send(c, (AHEAD,), c.x.at[1, :, hi], c.x.at[3, :, hi], c.minus)

    def partner_lo(c):
        arrived(c, (OWN, SIDE, 0), c.x.at[4, :, lo])
        send(c, (PARTNER, UPWARD, 0), c.x.at[4, :, lo], c.x.at[6, :, lo], c.plus)
        send(c, (PARTNER, DOWNWARD, 0), c.x.at[4, :, lo], c.x.at[5, :, lo], c.minus)

    def partner_hi(c):
        arrived(c, (OWN, SIDE, 1), c.x.at[4, :, hi])
        send(c, (PARTNER, DOWNWARD, 1), c.x.at[4, :, hi], c.x.at[5, :, hi], c.minus)
        send(c, (PARTNER, UPWARD, 1), c.x.at[4, :, hi], c.x.at[6, :, hi], c.plus)

    def partner_forward_up(c):
        arrived(c, (PARTNER, UPWARD, 0), c.x.at[6, :, lo])
        send(c, (PARTNER_AHEAD,), c.x.at[6, :, lo], c.x.at[7, :, lo], c.plus)

    def partner_forward_down(c):
        arrived(c, (PARTNER, DOWNWARD, 1), c.x.at[5, :, hi])
        send(c, (PARTNER_AHEAD,), c.x.at[5, :, hi], c.x.at[7, :, hi], c.minus)

    needs = {1: ((OWN, DOWNWARD, 0), lo), 2: ((OWN, UPWARD, 1), hi), 3: ((AHEAD,), None),
             5: ((PARTNER, DOWNWARD, 0), lo), 6: ((PARTNER, UPWARD, 1), hi), 7: ((PARTNER_AHEAD,), None)}
    begun = set()

    def multiply(c, j):
        if c.at not in begun:
            begun.add(c.at)
            for copy in (local[0], local[2]) if c is g else (local[1], local[3]):
                copy.wait()
            arrived(c, (BASIS,), c.w.at[hi])
        if j == 0 and c is a:
            arrived(c, (SWAP,), c.x.at[0, :, hi])
        if j in needs:
            name, cols = needs[j]
            arrived(c, name, c.x.at[j] if cols is None else c.x.at[j, :, cols])

        @pl.loop(0, WIDE // TILE)
        def _(n):
            cols = pl.ds(pl.multiple_of(n * TILE, TILE), TILE)
            c.p[j, :, cols] = jnp.dot(c.x[j], c.w[:, cols], preferred_element_type=F32)

        if j in ASIDE:
            for d in range(4):
                c.s1[j, d // 2, (first, second)[d % 2]] = encode(c.p[j, piece(c.q(d, 1))])
            send(c, (FIRST, j), c.s1.at[j], c.r1.at[j], c.sum_partner)
            return
        c.s1[j, UPWARD, first] = encode(c.p[j, piece(c.q(2, 0))])
        c.s1[j, UPWARD, second] = encode(c.p[j, piece(c.q(1, 1))])
        send(c, (FIRST, j), c.s1.at[j, UPWARD], c.r1.at[j, UPWARD], c.sum_plus)
        c.s1[j, DOWNWARD, first] = encode(c.p[j, piece(c.q(2, 1))])
        c.s1[j, DOWNWARD, second] = encode(c.p[j, piece(c.q(3, 0))])
        send(c, (FIRST, j), c.s1.at[j, DOWNWARD], c.r1.at[j, DOWNWARD], c.sum_minus)

    def sum_second(c, j):
        arrived(c, (FIRST, j), c.r1.at[j])
        if j in ASIDE:
            for d in range(4):
                at = piece(c.q(d, 0))
                c.p[j, at] = c.p[j, at] + decode(c.r1[j, d // 2, (first, second)[d % 2]])
            at = piece(c.q(2, 0))
            c.s2[j, UPWARD, :, lo] = encode(c.p[j, at, lo])
            c.s2[j, DOWNWARD, :, hi] = encode(c.p[j, at, hi])
            send(c, (SECOND, j), c.s2.at[j, UPWARD, :, lo], c.r2.at[j, UPWARD, :, lo], c.sum_plus)
            send(c, (SECOND, j), c.s2.at[j, DOWNWARD, :, hi], c.r2.at[j, DOWNWARD, :, hi], c.sum_minus)
            return
        c.s2[j, UPWARD] = encode(c.p[j, piece(c.q(1, 0))] + decode(c.r1[j, UPWARD, first]))
        send(c, (SECOND, j), c.s2.at[j, UPWARD], c.r2.at[j, UPWARD], c.sum_plus)
        c.s2[j, DOWNWARD] = encode(c.p[j, piece(c.q(3, 1))] + decode(c.r1[j, DOWNWARD, first]))
        send(c, (SECOND, j), c.s2.at[j, DOWNWARD], c.r2.at[j, DOWNWARD], c.sum_minus)

    def sum_partner(c, j):
        if j in ASIDE:
            arrived(c, (SECOND, j), c.r2.at[j, UPWARD])
            k = ASIDE.index(j)
            up, down = piece(c.q(1, 0)), piece(c.q(3, 0))
            c.s4[k, UPWARD, :, lo] = encode(c.p[j, up, lo] + decode(c.r2[j, UPWARD, :, lo]))
            c.s4[k, UPWARD, :, hi] = encode(c.p[j, up, hi])
            send(c, (THIRD, j), c.s4.at[k, UPWARD], c.r4.at[k, UPWARD], c.sum_plus)
            c.s4[k, DOWNWARD, :, lo] = encode(c.p[j, down, lo])
            c.s4[k, DOWNWARD, :, hi] = encode(c.p[j, down, hi] + decode(c.r2[j, DOWNWARD, :, hi]))
            send(c, (THIRD, j), c.s4.at[k, DOWNWARD], c.r4.at[k, DOWNWARD], c.sum_minus)
            return
        arrived(c, (SECOND, j), c.r2.at[j])
        c.s3[j] = encode(c.p[j, piece(c.q(0, 1))] + decode(c.r1[j, UPWARD, second]) + decode(c.r2[j, DOWNWARD]))
        send(c, (THIRD, j), c.s3.at[j], c.r3.at[j], c.sum_partner)
        at = piece(c.q(0, 0))
        c.p[j, at] = c.p[j, at] + decode(c.r1[j, DOWNWARD, second]) + decode(c.r2[j, UPWARD])

    def finish(c, j):
        at = piece(c.q(0, 0))
        if j in ASIDE:
            k = ASIDE.index(j)
            arrived(c, (THIRD, j), c.r4.at[k])
            c.rot[j, at] = (c.p[j, at] + decode(c.r4[k, UPWARD]) + decode(c.r4[k, DOWNWARD])).astype(BF16)
        else:
            arrived(c, (THIRD, j), c.r3.at[j])
            c.rot[j, at] = (c.p[j, at] + decode(c.r3[j])).astype(BF16)
        ref = c.rot.at[j, at]
        if j in DIRECT:
            send(c, (DONE, SIDE, j), ref, ref, c.sum_partner)
            for to in (c.sum_plus, c.sum_minus, c.sum_two):
                send(c, (DONE, j), ref, ref, to)
        else:
            send(c, (DONE, j), ref, ref, c.sum_plus)
            send(c, (DONE, j), ref, ref, c.sum_minus)
            send(c, (DONE, SIDE, j), ref, ref, c.sum_partner)

    def spread(c, j):
        arrived(c, (DONE, j), c.rot.at[j, pl.ds(0, 2 * PIECE)])
        ref = c.rot.at[j, piece(c.q(3, 0)), lo]
        send(c, (HALVES, j), ref, ref, c.sum_plus)
        ref = c.rot.at[j, piece(c.q(1, 0)), hi]
        send(c, (HALVES, j), ref, ref, c.sum_minus)
        if j in ASIDE:
            for d in (3, 1):
                ref = c.rot.at[j, piece(c.q(d, 0))]
                send(c, (DONE, SIDE, j), ref, ref, c.sum_partner)

    def across(c, j):
        if j in ASIDE:
            arrived(c, (HALVES, j), c.rot.at[j, first])
            ref = c.rot.at[j, piece(c.q(2, 0))]
            send(c, (DONE, SIDE, j), ref, ref, c.sum_partner)
            return
        arrived(c, (DONE, SIDE, j), c.rot.at[j, first])
        ref = c.rot.at[j, piece(c.q(0, 1))]
        if j in DIRECT:
            for to in (c.sum_two, c.sum_plus, c.sum_minus):
                send(c, (HALVES, j), ref, ref, to)
        else:
            send(c, (ACROSS, j), ref, ref, c.sum_plus)
            send(c, (ACROSS, j), ref, ref, c.sum_minus)

    def spread_across(c, j):
        arrived(c, (ACROSS, j), c.rot.at[j, pl.ds(0, 2 * PIECE)])
        ref = c.rot.at[j, piece(c.q(3, 1)), lo]
        send(c, (HALVES, j), ref, ref, c.sum_plus)
        ref = c.rot.at[j, piece(c.q(1, 1)), hi]
        send(c, (HALVES, j), ref, ref, c.sum_minus)

    def share_rows(c, j, rows):
        if c is a:
            send(c, (SHARED, j), rot_a.at[j, rows], rot_ao.at[j, rows], other)
        else:
            send(c, (SHARED, j), rot_g.at[j, rows, hi], rot_go.at[j, rows], other)

    def share_early(c, j):
        arrived(c, (DONE, j), c.rot.at[j, pl.ds(0, 3 * PIECE)])
        for d in range(4):
            share_rows(c, j, piece(c.q(d, 0)))

    def share(c, j):
        if j in DIRECT:
            arrived(c, (HALVES, j), c.rot.at[j, pl.ds(0, 3 * PIECE)])
            for d in range(4):
                share_rows(c, j, piece(c.q(d, 1)))
            return
        if j in ASIDE:
            arrived(c, (DONE, SIDE, j), c.rot.at[j, pl.ds(0, 4 * PIECE)])
        else:
            arrived(c, (HALVES, j), c.rot.at[j, pl.ds(0, 2 * PIECE)])
        share_rows(c, j, pl.ds(0, HALF))

    def receive(c, j):
        arrived(c, (SHARED, j), rot_ao.at[j] if c is a else rot_go.at[j])

    def ring_slot(up):
        return up + (up // 2) * (1 - 2 * (up % 2))

    def a_slot(t):
        return ring_slot((t % 4 + 4 - x) % 4) + 4 * ((t // 4 + yh) % 2)

    def g_slot(t):
        return ring_slot((t // 2 + 4 - z) % 4) + 4 * ((t + yl) % 2)

    def correlate(above, upto):
        @pl.loop(0, SLOTS)
        def _(t):
            last = jnp.maximum(a_slot(t), g_slot(t))

            @pl.when((last > above) & (last <= upto))
            def _():
                rows = jnp.concatenate([rot_g[g_slot(t), :, lo], rot_go[g_slot(t)]], axis=0)
                columns = jnp.concatenate([rot_a[a_slot(t)], rot_ao[a_slot(t)]], axis=0)
                out[t // 4] += lax.dot_general(
                    rows, columns, (((0,), (0,)), ((), ())), preferred_element_type=F32)

    steps = (own, forward_up, forward_down, partner_lo, partner_hi, partner_forward_up, partner_forward_down,
             multiply, sum_second, sum_partner, finish, spread, across, spread_across, share, receive, share_early)
    levels = (-1, 0, 1, 2, 3, 4, 5, 6, 7)
    for code in ORDER:
        c, step, j = (g, a)[code // 1000], code % 1000 // 10, code % 10
        if step < 7:
            steps[step](c)
        elif step < len(steps):
            steps[step](c, j)
        else:
            correlate(levels[j], levels[j + 1])
    pltpu.make_async_copy(total, total, send_sem).wait()


def on_device(acts, grads, qa, qs):
    vm = pltpu.VMEM
    sums = [vm((SLOTS, 2, 2 * PIECE, WIDE), BF16)] * 2 + [vm((SLOTS, 2, PIECE, WIDE), BF16)] * 2
    sums += [vm((SLOTS, PIECE, WIDE), BF16)] * 2 + [vm((max(len(ASIDE), 1), 2, PIECE, WIDE), BF16)] * 2
    args = [pltpu.with_memory_space_constraint(v, pltpu.HBM) for v in (acts, grads, qa, qs)]
    blocks, _ = pl.pallas_call(
        kernel,
        out_shape=(jax.ShapeDtypeStruct((SEQS, NARROW, WIDE), F32), pltpu.HBM((SENT, WIDE), BF16)),
        in_specs=[pl.BlockSpec(memory_space=pl.ANY)] * 4,
        out_specs=(pl.BlockSpec(memory_space=pltpu.VMEM), pl.BlockSpec(memory_space=pltpu.HBM)),
        scratch_shapes=[
            vm((SLOTS, HALF, WIDE), BF16), vm((SLOTS, HALF, WIDE), BF16),
            vm((WIDE, WIDE), BF16), vm((WIDE, WIDE), BF16),
            vm((SLOTS, HALF, WIDE), F32), vm((SLOTS, HALF, WIDE), F32),
            vm((SLOTS, HALF, WIDE), BF16), vm((SLOTS, HALF, WIDE), BF16),
            vm((SLOTS, HALF, WIDE), BF16), vm((SLOTS, HALF, NARROW), BF16),
            *sums, *sums,
            pltpu.SemaphoreType.DMA((4,)),
            pltpu.SemaphoreType.DMA, pltpu.SemaphoreType.DMA((ARRIVALS,)),
        ],
        compiler_params=pltpu.CompilerParams(
            collective_id=0, has_side_effects=True, vmem_limit_bytes=44 * 2 ** 20),
        cost_estimate=pl.CostEstimate(flops=6442450944, bytes_accessed=5 * 2 ** 20, transcendentals=0),
        name="rotate_and_correlate",
    )(*args)
    return (blocks[0] * blocks[0] + blocks[1] * blocks[1]) * (1.0 / TOKENS)


def solution(mesh):
    return jax.shard_map(
        on_device,
        mesh=mesh,
        in_specs=(P("row", "col"), P("col", "row"), P("col", "row"), P("row", "col")),
        out_specs=P("col", "row"),
        check_vma=False,
    )
```

```python
import jax
import jax.numpy as jnp
from jax import lax
from jax.experimental import pallas as pl
from jax.experimental.pallas import tpu as pltpu
from jax.sharding import PartitionSpec as P

MESH = pl.DeviceIdType.MESH
F32, BF16 = jnp.float32, jnp.bfloat16

TOKENS, D, SEQS = 2048, 8192, 2
SLOTS = 8
HALF = TOKENS // SLOTS // 2
PIECE = HALF // SLOTS
WIDE = 1024
NARROW = WIDE // 2
TILE = 512
DIRECT = (6, 7)
ASIDE = (3,)
ARRIVALS = 149
SENT = 8000

PASSES = ((-1, 0), (0, 2), (2, 4), (4, 6), (6, 7))

UP = 2.0 ** 30

ORDER = (
    0, 1000, 70, 1070, 1010, 10, 1020, 20, 71, 30, 1080, 80, 72, 40, 74, 1073, 1071, 81, 1072, 1030, 1090, 73, 1040,
    82, 1074, 1083, 1081, 50, 60, 84, 75, 91, 76, 1082, 90, 1100, 83, 1091, 92, 1084, 1050, 1060, 1075, 94, 100, 1076,
    85, 1092, 1093, 101, 1120, 86, 1094, 1101, 77, 104, 1085, 1102, 102, 121, 1086, 1103, 1077, 95, 1104, 96, 93,
    1095, 87, 1121, 1122, 120, 1110, 1096, 122, 1113, 105, 1087, 111, 1112, 103, 1114, 124, 1111, 1124, 1105, 110,
    1130, 97, 1106, 131, 106, 130, 1131, 1097, 132, 113, 112, 114, 1125, 134, 1123, 1132, 125, 1134, 141, 1140, 1126,
    107, 1107, 126, 123, 1166, 1135, 1142, 142, 1144, 140, 144, 1115, 1141, 115, 135, 1127, 127, 1143, 150, 1150, 170,
    1152, 143, 152, 151, 167, 166, 1145, 154, 1151, 1146, 171, 146, 145, 1167, 1154, 153, 1153, 172, 1147, 156, 1156,
    1155, 147, 155, 173, 157, 1157, 174,
)


def encode(v):
    v = v * UP
    return (v * v * v).astype(BF16)


def decode(c):
    c = c.astype(F32)
    size = jnp.maximum(jnp.abs(c), 2.0 ** -126)
    return c * (jnp.exp2(jnp.log2(size) * (-2.0 / 3.0)) * (1.0 / UP))


class Chain:
    def __init__(self, **refs):
        self.__dict__.update(refs)


def kernel(acts, grads, qa, qs, out, total,
           sums, xa, xg, wa, wg, pa, pg, rot_a, rot_g, rot_ao, rot_go,
           s1a, r1a, s2a, r2a, s3a, r3a, s4a, r4a, s1g, r1g, s2g, r2g, s3g, r3g, s4g, r4g,
           local_sem, send_sem, recv_sem):
    row, col = lax.axis_index("row"), lax.axis_index("col")
    yh, x = row // 4, row % 4
    z, yl, h = col // 4, (col // 2) % 2, col % 2

    def dev(dyh, dx, dz, dyl, core):
        return ((yh + dyh) % 2 * 4 + (x + dx) % 4, (z + dz) % 4 * 4 + (yl + dyl) % 2 * 2 + core)

    x_plus, x_minus = dev(0, 1, 0, 0, h), dev(0, 3, 0, 0, h)
    z_plus, z_minus = dev(0, 0, 1, 0, h), dev(0, 0, 3, 0, h)
    y_far, y_near = dev(1, 0, 0, 0, h), dev(0, 0, 0, 1, h)
    other = dev(0, 0, 0, 0, 1 - h)
    x_plus_o, x_minus_o, y_far_o = dev(0, 1, 0, 0, 1 - h), dev(0, 3, 0, 0, 1 - h), dev(1, 0, 0, 0, 1 - h)

    barrier = pltpu.get_barrier_semaphore()
    x_two, z_two = dev(0, 2, 0, 0, h), dev(0, 0, 2, 0, h)
    neighbours = (x_plus, x_minus, z_plus, z_minus, y_far, y_near, other, x_plus_o, x_minus_o, y_far_o, x_two, z_two)
    for n in neighbours:
        pl.semaphore_signal(barrier, inc=1, device_id=n, device_id_type=MESH)

    names = {}

    def arrival(c, name):
        return recv_sem.at[names.setdefault((c.at,) + name, len(names))]

    def send(c, name, src, dst, to):
        pltpu.make_async_remote_copy(
            src_ref=src, dst_ref=dst, send_sem=send_sem, recv_sem=arrival(c, name),
            device_id=to, device_id_type=MESH).start()

    def arrived(c, name, ref):
        pltpu.make_async_remote_copy(
            src_ref=ref, dst_ref=ref, send_sem=send_sem, recv_sem=arrival(c, name),
            device_id=other, device_id_type=MESH).wait_recv()

    def piece(q):
        return pl.ds(pl.multiple_of(q * PIECE, PIECE), PIECE)

    lo, hi = pl.ds(0, NARROW), pl.ds(NARROW, NARROW)
    mine = pl.ds(pl.multiple_of(h * HALF, HALF), HALF)
    its = pl.ds(pl.multiple_of((1 - h) * HALF, HALF), HALF)
    first, second = pl.ds(0, PIECE), pl.ds(PIECE, PIECE)

    a = Chain(at=1, plus=x_plus, minus=x_minus, partner=y_far,
              sum_plus=z_plus, sum_minus=z_minus, sum_two=z_two, sum_partner=y_near,
              plus_o=x_plus_o, minus_o=x_minus_o, partner_o=y_far_o,
              own_lo=acts.at[mine], own_hi=acts.at[its],
              q=lambda d, e: ((z + d) % 4) * 2 + (yl + e) % 2,
              x=xa, w=wa, p=pa, rot=rot_a, s1=s1a, r1=r1a, s2=s2a, r2=r2a, s3=s3a, r3=r3a,
              s4=s4a, r4=r4a)
    g = Chain(at=0, plus=z_plus, minus=z_minus, partner=y_near,
              sum_plus=x_plus, sum_minus=x_minus, sum_two=x_two, sum_partner=y_far,
              plus_o=z_plus, minus_o=z_minus, partner_o=y_near,
              own_lo=grads.at[:, lo], own_hi=grads.at[:, hi],
              q=lambda d, e: ((yh + e) % 2) * 4 + (x + d) % 4,
              x=xg, w=wg, p=pg, rot=rot_g, s1=s1g, r1=r1g, s2=s2g, r2=r2g, s3=s3g, r3=r3g,
              s4=s4g, r4=r4g)

    local = [
        pltpu.make_async_copy(grads, xg.at[0], local_sem.at[0]),
        pltpu.make_async_copy(acts.at[mine], xa.at[0, :, lo], local_sem.at[1]),
        pltpu.make_async_copy(qs, wg.at[:, lo], local_sem.at[2]),
        pltpu.make_async_copy(qa, wa.at[lo], local_sem.at[3]),
    ]
    for copy in local:
        copy.start()

    pl.semaphore_wait(barrier, len(neighbours))

    UPWARD, DOWNWARD, SIDE = 0, 1, 2
    OWN, AHEAD, PARTNER, PARTNER_AHEAD, SWAP, BASIS, FIRST, SECOND, THIRD, DONE, ACROSS, HALVES, SHARED = range(13)

    def own(c):
        send(c, (OWN, UPWARD, 0), c.own_lo, c.x.at[2, :, lo], c.plus)
        send(c, (OWN, DOWNWARD, 1), c.own_hi, c.x.at[1, :, hi], c.minus_o)
        send(c, (OWN, SIDE, 0), c.own_lo, c.x.at[4, :, lo], c.partner)
        send(c, (OWN, UPWARD, 1), c.own_hi, c.x.at[2, :, hi], c.plus_o)
        send(c, (OWN, DOWNWARD, 0), c.own_lo, c.x.at[1, :, lo], c.minus)
        send(c, (OWN, SIDE, 1), c.own_hi, c.x.at[4, :, hi], c.partner_o)
        if c is a:
            send(c, (SWAP,), acts.at[its], xa.at[0, :, hi], other)
            send(c, (BASIS,), qa, wa.at[hi], other)
            sums[...] = jnp.zeros_like(sums)
        else:
            send(c, (BASIS,), qs, wg.at[:, hi], other)

    def forward_up(c):
        arrived(c, (OWN, UPWARD, 0), c.x.at[2, :, lo])
        send(c, (AHEAD,), c.x.at[2, :, lo], c.x.at[3, :, lo], c.plus)

    def forward_down(c):
        arrived(c, (OWN, DOWNWARD, 1), c.x.at[1, :, hi])
        send(c, (AHEAD,), c.x.at[1, :, hi], c.x.at[3, :, hi], c.minus)

    def partner_lo(c):
        arrived(c, (OWN, SIDE, 0), c.x.at[4, :, lo])
        send(c, (PARTNER, UPWARD, 0), c.x.at[4, :, lo], c.x.at[6, :, lo], c.plus)
        send(c, (PARTNER, DOWNWARD, 0), c.x.at[4, :, lo], c.x.at[5, :, lo], c.minus)

    def partner_hi(c):
        arrived(c, (OWN, SIDE, 1), c.x.at[4, :, hi])
        send(c, (PARTNER, DOWNWARD, 1), c.x.at[4, :, hi], c.x.at[5, :, hi], c.minus)
        send(c, (PARTNER, UPWARD, 1), c.x.at[4, :, hi], c.x.at[6, :, hi], c.plus)

    def partner_forward_up(c):
        arrived(c, (PARTNER, UPWARD, 0), c.x.at[6, :, lo])
        send(c, (PARTNER_AHEAD,), c.x.at[6, :, lo], c.x.at[7, :, lo], c.plus)

    def partner_forward_down(c):
        arrived(c, (PARTNER, DOWNWARD, 1), c.x.at[5, :, hi])
        send(c, (PARTNER_AHEAD,), c.x.at[5, :, hi], c.x.at[7, :, hi], c.minus)

    needs = {1: ((OWN, DOWNWARD, 0), lo), 2: ((OWN, UPWARD, 1), hi), 3: ((AHEAD,), None),
             5: ((PARTNER, DOWNWARD, 0), lo), 6: ((PARTNER, UPWARD, 1), hi), 7: ((PARTNER_AHEAD,), None)}
    begun = set()

    def multiply(c, j):
        if c.at not in begun:
            begun.add(c.at)
            for copy in (local[0], local[2]) if c is g else (local[1], local[3]):
                copy.wait()
            arrived(c, (BASIS,), c.w.at[hi])
        if j == 0 and c is a:
            arrived(c, (SWAP,), c.x.at[0, :, hi])
        if j in needs:
            name, cols = needs[j]
            arrived(c, name, c.x.at[j] if cols is None else c.x.at[j, :, cols])

        @pl.loop(0, WIDE // TILE)
        def _(n):
            cols = pl.ds(pl.multiple_of(n * TILE, TILE), TILE)
            c.p[j, :, cols] = jnp.dot(c.x[j], c.w[:, cols], preferred_element_type=F32)

        if j in ASIDE:
            for d in range(4):
                c.s1[j, d // 2, (first, second)[d % 2]] = encode(c.p[j, piece(c.q(d, 1))])
            send(c, (FIRST, j), c.s1.at[j], c.r1.at[j], c.sum_partner)
            return
        c.s1[j, UPWARD, first] = encode(c.p[j, piece(c.q(2, 0))])
        c.s1[j, UPWARD, second] = encode(c.p[j, piece(c.q(1, 1))])
        send(c, (FIRST, j), c.s1.at[j, UPWARD], c.r1.at[j, UPWARD], c.sum_plus)
        c.s1[j, DOWNWARD, first] = encode(c.p[j, piece(c.q(2, 1))])
        c.s1[j, DOWNWARD, second] = encode(c.p[j, piece(c.q(3, 0))])
        send(c, (FIRST, j), c.s1.at[j, DOWNWARD], c.r1.at[j, DOWNWARD], c.sum_minus)

    def sum_second(c, j):
        arrived(c, (FIRST, j), c.r1.at[j])
        if j in ASIDE:
            for d in range(4):
                at = piece(c.q(d, 0))
                c.p[j, at] = c.p[j, at] + decode(c.r1[j, d // 2, (first, second)[d % 2]])
            at = piece(c.q(2, 0))
            c.s2[j, UPWARD, :, lo] = encode(c.p[j, at, lo])
            c.s2[j, DOWNWARD, :, hi] = encode(c.p[j, at, hi])
            send(c, (SECOND, j), c.s2.at[j, UPWARD, :, lo], c.r2.at[j, UPWARD, :, lo], c.sum_plus)
            send(c, (SECOND, j), c.s2.at[j, DOWNWARD, :, hi], c.r2.at[j, DOWNWARD, :, hi], c.sum_minus)
            return
        c.s2[j, UPWARD] = encode(c.p[j, piece(c.q(1, 0))] + decode(c.r1[j, UPWARD, first]))
        send(c, (SECOND, j), c.s2.at[j, UPWARD], c.r2.at[j, UPWARD], c.sum_plus)
        c.s2[j, DOWNWARD] = encode(c.p[j, piece(c.q(3, 1))] + decode(c.r1[j, DOWNWARD, first]))
        send(c, (SECOND, j), c.s2.at[j, DOWNWARD], c.r2.at[j, DOWNWARD], c.sum_minus)

    def sum_partner(c, j):
        if j in ASIDE:
            arrived(c, (SECOND, j), c.r2.at[j, UPWARD])
            k = ASIDE.index(j)
            up, down = piece(c.q(1, 0)), piece(c.q(3, 0))
            c.s4[k, UPWARD, :, lo] = encode(c.p[j, up, lo] + decode(c.r2[j, UPWARD, :, lo]))
            c.s4[k, UPWARD, :, hi] = encode(c.p[j, up, hi])
            send(c, (THIRD, j), c.s4.at[k, UPWARD], c.r4.at[k, UPWARD], c.sum_plus)
            c.s4[k, DOWNWARD, :, lo] = encode(c.p[j, down, lo])
            c.s4[k, DOWNWARD, :, hi] = encode(c.p[j, down, hi] + decode(c.r2[j, DOWNWARD, :, hi]))
            send(c, (THIRD, j), c.s4.at[k, DOWNWARD], c.r4.at[k, DOWNWARD], c.sum_minus)
            return
        arrived(c, (SECOND, j), c.r2.at[j])
        c.s3[j] = encode(c.p[j, piece(c.q(0, 1))] + decode(c.r1[j, UPWARD, second]) + decode(c.r2[j, DOWNWARD]))
        send(c, (THIRD, j), c.s3.at[j], c.r3.at[j], c.sum_partner)
        at = piece(c.q(0, 0))
        c.p[j, at] = c.p[j, at] + decode(c.r1[j, DOWNWARD, second]) + decode(c.r2[j, UPWARD])

    def finish(c, j):
        at = piece(c.q(0, 0))
        if j in ASIDE:
            k = ASIDE.index(j)
            arrived(c, (THIRD, j), c.r4.at[k])
            c.rot[j, at] = (c.p[j, at] + decode(c.r4[k, UPWARD]) + decode(c.r4[k, DOWNWARD])).astype(BF16)
        else:
            arrived(c, (THIRD, j), c.r3.at[j])
            c.rot[j, at] = (c.p[j, at] + decode(c.r3[j])).astype(BF16)
        ref = c.rot.at[j, at]
        if j in DIRECT:
            send(c, (DONE, SIDE, j), ref, ref, c.sum_partner)
            for to in (c.sum_plus, c.sum_minus, c.sum_two):
                send(c, (DONE, j), ref, ref, to)
        else:
            send(c, (DONE, j), ref, ref, c.sum_plus)
            send(c, (DONE, j), ref, ref, c.sum_minus)
            send(c, (DONE, SIDE, j), ref, ref, c.sum_partner)

    def spread(c, j):
        arrived(c, (DONE, j), c.rot.at[j, pl.ds(0, 2 * PIECE)])
        ref = c.rot.at[j, piece(c.q(3, 0)), lo]
        send(c, (HALVES, j), ref, ref, c.sum_plus)
        ref = c.rot.at[j, piece(c.q(1, 0)), hi]
        send(c, (HALVES, j), ref, ref, c.sum_minus)
        if j in ASIDE:
            for d in (3, 1):
                ref = c.rot.at[j, piece(c.q(d, 0))]
                send(c, (DONE, SIDE, j), ref, ref, c.sum_partner)

    def across(c, j):
        if j in ASIDE:
            arrived(c, (HALVES, j), c.rot.at[j, first])
            ref = c.rot.at[j, piece(c.q(2, 0))]
            send(c, (DONE, SIDE, j), ref, ref, c.sum_partner)
            return
        arrived(c, (DONE, SIDE, j), c.rot.at[j, first])
        ref = c.rot.at[j, piece(c.q(0, 1))]
        if j in DIRECT:
            for to in (c.sum_two, c.sum_plus, c.sum_minus):
                send(c, (HALVES, j), ref, ref, to)
        else:
            send(c, (ACROSS, j), ref, ref, c.sum_plus)
            send(c, (ACROSS, j), ref, ref, c.sum_minus)

    def spread_across(c, j):
        arrived(c, (ACROSS, j), c.rot.at[j, pl.ds(0, 2 * PIECE)])
        ref = c.rot.at[j, piece(c.q(3, 1)), lo]
        send(c, (HALVES, j), ref, ref, c.sum_plus)
        ref = c.rot.at[j, piece(c.q(1, 1)), hi]
        send(c, (HALVES, j), ref, ref, c.sum_minus)

    def share_rows(c, j, rows):
        if c is a:
            send(c, (SHARED, j), rot_a.at[j, rows], rot_ao.at[j, rows], other)
        else:
            send(c, (SHARED, j), rot_g.at[j, rows, hi], rot_go.at[j, rows], other)

    def share_early(c, j):
        arrived(c, (DONE, j), c.rot.at[j, pl.ds(0, 3 * PIECE)])
        for d in range(4):
            share_rows(c, j, piece(c.q(d, 0)))

    def share(c, j):
        if j in DIRECT:
            arrived(c, (HALVES, j), c.rot.at[j, pl.ds(0, 3 * PIECE)])
            for d in range(4):
                share_rows(c, j, piece(c.q(d, 1)))
            return
        if j in ASIDE:
            arrived(c, (DONE, SIDE, j), c.rot.at[j, pl.ds(0, 4 * PIECE)])
        else:
            arrived(c, (HALVES, j), c.rot.at[j, pl.ds(0, 2 * PIECE)])
        share_rows(c, j, pl.ds(0, HALF))

    def receive(c, j):
        arrived(c, (SHARED, j), rot_ao.at[j] if c is a else rot_go.at[j])

    def ring_slot(up):
        return up + (up // 2) * (1 - 2 * (up % 2))

    def a_slot(t):
        return ring_slot((t % 4 + 4 - x) % 4) + 4 * ((t // 4 + yh) % 2)

    def g_slot(t):
        return ring_slot((t // 2 + 4 - z) % 4) + 4 * ((t + yl) % 2)

    def correlate(above, upto):
        @pl.loop(0, SLOTS)
        def _(t):
            last = jnp.maximum(a_slot(t), g_slot(t))

            @pl.when((last > above) & (last <= upto))
            def _():
                rows = jnp.concatenate([rot_g[g_slot(t), :, lo], rot_go[g_slot(t)]], axis=0)
                columns = jnp.concatenate([rot_a[a_slot(t)], rot_ao[a_slot(t)]], axis=0)
                sums[t // 4] += lax.dot_general(
                    rows, columns, (((0,), (0,)), ((), ())), preferred_element_type=F32)

    steps = (own, forward_up, forward_down, partner_lo, partner_hi, partner_forward_up, partner_forward_down,
             multiply, sum_second, sum_partner, finish, spread, across, spread_across, share, receive, share_early)
    for code in ORDER:
        c, step, j = (g, a)[code // 1000], code % 1000 // 10, code % 10
        if step < 7:
            steps[step](c)
        elif step < len(steps):
            steps[step](c, j)
        else:
            correlate(*PASSES[j])

    @pl.loop(0, NARROW // 64)
    def _(n):
        rows = pl.ds(pl.multiple_of(n * 64, 64), 64)
        out[rows] = (sums[0, rows] * sums[0, rows] + sums[1, rows] * sums[1, rows]) * (1.0 / TOKENS)

    assert len(names) == ARRIVALS
    pltpu.make_async_copy(total, total, send_sem).wait()


def on_device(acts, grads, qa, qs):
    vm = pltpu.VMEM
    sums = [vm((SLOTS, 2, 2 * PIECE, WIDE), BF16)] * 2 + [vm((SLOTS, 2, PIECE, WIDE), BF16)] * 2
    sums += [vm((SLOTS, PIECE, WIDE), BF16)] * 2 + [vm((max(len(ASIDE), 1), 2, PIECE, WIDE), BF16)] * 2
    args = [pltpu.with_memory_space_constraint(v, pltpu.HBM) for v in (acts, grads, qa, qs)]
    correction, _ = pl.pallas_call(
        kernel,
        out_shape=(jax.ShapeDtypeStruct((NARROW, WIDE), F32), pltpu.HBM((SENT, WIDE), BF16)),
        in_specs=[pl.BlockSpec(memory_space=pl.ANY)] * 4,
        out_specs=(pl.BlockSpec(memory_space=pltpu.VMEM), pl.BlockSpec(memory_space=pltpu.HBM)),
        scratch_shapes=[
            vm((SEQS, NARROW, WIDE), F32),
            vm((SLOTS, HALF, WIDE), BF16), vm((SLOTS, HALF, WIDE), BF16),
            vm((WIDE, WIDE), BF16), vm((WIDE, WIDE), BF16),
            vm((SLOTS, HALF, WIDE), F32), vm((SLOTS, HALF, WIDE), F32),
            vm((SLOTS, HALF, WIDE), BF16), vm((SLOTS, HALF, WIDE), BF16),
            vm((SLOTS, HALF, WIDE), BF16), vm((SLOTS, HALF, NARROW), BF16),
            *sums, *sums,
            pltpu.SemaphoreType.DMA((4,)),
            pltpu.SemaphoreType.DMA, pltpu.SemaphoreType.DMA((ARRIVALS,)),
        ],
        compiler_params=pltpu.CompilerParams(
            collective_id=0, has_side_effects=True, vmem_limit_bytes=48 * 2 ** 20),
        cost_estimate=pl.CostEstimate(flops=6442450944, bytes_accessed=5 * 2 ** 20, transcendentals=0),
        name="rotate_and_correlate",
    )(*args)
    return correction


def solution(mesh):
    return jax.shard_map(
        on_device,
        mesh=mesh,
        in_specs=(P("row", "col"), P("col", "row"), P("col", "row"), P("row", "col")),
        out_specs=P("col", "row"),
        check_vma=False,
    )
```

```python
import jax
import jax.numpy as jnp
from jax import lax
from jax.experimental import pallas as pl
from jax.experimental.pallas import tpu as pltpu
from jax.sharding import PartitionSpec as P

MESH = pl.DeviceIdType.MESH
F32, BF16 = jnp.float32, jnp.bfloat16

TOKENS, D, SEQS = 2048, 8192, 2
SLOTS = 8
HALF = TOKENS // SLOTS // 2
PIECE = HALF // SLOTS
WIDE = 1024
NARROW = WIDE // 2
TILE = 512
DIRECT = (6, 7)
ASIDE = (2, 3)
LATER = (3,)
ARRIVALS = 149
SENT = 8000

PASSES = ((-1, 0), (0, 2), (2, 4), (4, 6), (6, 7))

UP = 2.0 ** 30

ORDER = (
    0, 1000, 1070, 70, 20, 1020, 1010, 30, 1071, 71, 10, 72, 40, 80, 1030, 1072, 74, 1040, 1074, 1073, 1081, 1080, 81,
    73, 50, 60, 75, 1084, 84, 1050, 90, 82, 1060, 1082, 1090, 1083, 1091, 1075, 91, 1076, 85, 94, 77, 1094, 83, 1100,
    76, 1093, 1092, 1101, 100, 95, 101, 1085, 92, 1077, 1086, 104, 1104, 1102, 1103, 93, 86, 87, 1095, 105, 1121, 121,
    102, 1087, 1096, 1120, 1122, 103, 124, 96, 111, 1124, 120, 1105, 1111, 110, 1112, 97, 1131, 125, 131, 1106, 1097,
    122, 1132, 1110, 113, 106, 130, 1113, 1114, 1130, 1125, 1134, 112, 1126, 107, 132, 134, 114, 141, 115, 1107, 135,
    1142, 123, 1123, 1140, 1141, 1135, 126, 1166, 140, 1115, 1144, 1146, 127, 1127, 151, 1152, 142, 144, 143, 1151,
    1143, 145, 1150, 150, 1154, 170, 1145, 152, 171, 166, 154, 146, 153, 1156, 167, 1167, 1153, 172, 1147, 1155, 155,
    147, 156, 173, 157, 1157, 174,
)


def encode(v):
    v = v * UP
    return (v * v * v).astype(BF16)


def decode(c):
    c = c.astype(F32)
    size = jnp.maximum(jnp.abs(c), 2.0 ** -126)
    return c * (jnp.exp2(jnp.log2(size) * (-2.0 / 3.0)) * (1.0 / UP))


class Chain:
    def __init__(self, **refs):
        self.__dict__.update(refs)


def kernel(acts, grads, qa, qs, out, total,
           sums, xa, xg, wa, wg, pa, pg, rot_a, rot_g, rot_ao, rot_go,
           s1a, r1a, s2a, r2a, s3a, r3a, s4a, r4a, s1g, r1g, s2g, r2g, s3g, r3g, s4g, r4g,
           local_sem, send_sem, recv_sem):
    row, col = lax.axis_index("row"), lax.axis_index("col")
    yh, x = row // 4, row % 4
    z, yl, h = col // 4, (col // 2) % 2, col % 2

    def dev(dyh, dx, dz, dyl, core):
        return ((yh + dyh) % 2 * 4 + (x + dx) % 4, (z + dz) % 4 * 4 + (yl + dyl) % 2 * 2 + core)

    x_plus, x_minus = dev(0, 1, 0, 0, h), dev(0, 3, 0, 0, h)
    z_plus, z_minus = dev(0, 0, 1, 0, h), dev(0, 0, 3, 0, h)
    y_far, y_near = dev(1, 0, 0, 0, h), dev(0, 0, 0, 1, h)
    other = dev(0, 0, 0, 0, 1 - h)
    x_plus_o, x_minus_o, y_far_o = dev(0, 1, 0, 0, 1 - h), dev(0, 3, 0, 0, 1 - h), dev(1, 0, 0, 0, 1 - h)

    barrier = pltpu.get_barrier_semaphore()
    x_two, z_two = dev(0, 2, 0, 0, h), dev(0, 0, 2, 0, h)
    neighbours = (x_plus, x_minus, z_plus, z_minus, y_far, y_near, other, x_plus_o, x_minus_o, y_far_o, x_two, z_two)
    for n in neighbours:
        pl.semaphore_signal(barrier, inc=1, device_id=n, device_id_type=MESH)

    names = {}

    def arrival(c, name):
        return recv_sem.at[names.setdefault((c.at,) + name, len(names))]

    def send(c, name, src, dst, to):
        pltpu.make_async_remote_copy(
            src_ref=src, dst_ref=dst, send_sem=send_sem, recv_sem=arrival(c, name),
            device_id=to, device_id_type=MESH).start()

    def arrived(c, name, ref):
        pltpu.make_async_remote_copy(
            src_ref=ref, dst_ref=ref, send_sem=send_sem, recv_sem=arrival(c, name),
            device_id=other, device_id_type=MESH).wait_recv()

    def piece(q):
        return pl.ds(pl.multiple_of(q * PIECE, PIECE), PIECE)

    lo, hi = pl.ds(0, NARROW), pl.ds(NARROW, NARROW)
    mine = pl.ds(pl.multiple_of(h * HALF, HALF), HALF)
    its = pl.ds(pl.multiple_of((1 - h) * HALF, HALF), HALF)
    first, second = pl.ds(0, PIECE), pl.ds(PIECE, PIECE)

    a = Chain(at=1, plus=x_plus, minus=x_minus, partner=y_far,
              sum_plus=z_plus, sum_minus=z_minus, sum_two=z_two, sum_partner=y_near,
              plus_o=x_plus_o, minus_o=x_minus_o, partner_o=y_far_o,
              own_lo=acts.at[mine], own_hi=acts.at[its],
              q=lambda d, e: ((z + d) % 4) * 2 + (yl + e) % 2,
              x=xa, w=wa, p=pa, rot=rot_a, s1=s1a, r1=r1a, s2=s2a, r2=r2a, s3=s3a, r3=r3a,
              s4=s4a, r4=r4a)
    g = Chain(at=0, plus=z_plus, minus=z_minus, partner=y_near,
              sum_plus=x_plus, sum_minus=x_minus, sum_two=x_two, sum_partner=y_far,
              plus_o=z_plus, minus_o=z_minus, partner_o=y_near,
              own_lo=grads.at[:, lo], own_hi=grads.at[:, hi],
              q=lambda d, e: ((yh + e) % 2) * 4 + (x + d) % 4,
              x=xg, w=wg, p=pg, rot=rot_g, s1=s1g, r1=r1g, s2=s2g, r2=r2g, s3=s3g, r3=r3g,
              s4=s4g, r4=r4g)

    local = [
        pltpu.make_async_copy(grads, xg.at[0], local_sem.at[0]),
        pltpu.make_async_copy(acts.at[mine], xa.at[0, :, lo], local_sem.at[1]),
        pltpu.make_async_copy(qs, wg.at[:, lo], local_sem.at[2]),
        pltpu.make_async_copy(qa, wa.at[lo], local_sem.at[3]),
    ]
    for copy in local:
        copy.start()

    pl.semaphore_wait(barrier, len(neighbours))

    UPWARD, DOWNWARD, SIDE = 0, 1, 2
    OWN, AHEAD, PARTNER, PARTNER_AHEAD, SWAP, BASIS, FIRST, SECOND, THIRD, DONE, ACROSS, HALVES, SHARED = range(13)

    def own(c):
        send(c, (OWN, UPWARD, 0), c.own_lo, c.x.at[2, :, lo], c.plus)
        send(c, (OWN, DOWNWARD, 1), c.own_hi, c.x.at[1, :, hi], c.minus_o)
        send(c, (OWN, SIDE, 0), c.own_lo, c.x.at[4, :, lo], c.partner)
        send(c, (OWN, UPWARD, 1), c.own_hi, c.x.at[2, :, hi], c.plus_o)
        send(c, (OWN, DOWNWARD, 0), c.own_lo, c.x.at[1, :, lo], c.minus)
        send(c, (OWN, SIDE, 1), c.own_hi, c.x.at[4, :, hi], c.partner_o)
        if c is a:
            send(c, (SWAP,), acts.at[its], xa.at[0, :, hi], other)
            send(c, (BASIS,), qa, wa.at[hi], other)
            sums[...] = jnp.zeros_like(sums)
        else:
            send(c, (BASIS,), qs, wg.at[:, hi], other)

    def forward_up(c):
        arrived(c, (OWN, UPWARD, 0), c.x.at[2, :, lo])
        send(c, (AHEAD,), c.x.at[2, :, lo], c.x.at[3, :, lo], c.plus)

    def forward_down(c):
        arrived(c, (OWN, DOWNWARD, 1), c.x.at[1, :, hi])
        send(c, (AHEAD,), c.x.at[1, :, hi], c.x.at[3, :, hi], c.minus)

    def partner_lo(c):
        arrived(c, (OWN, SIDE, 0), c.x.at[4, :, lo])
        send(c, (PARTNER, UPWARD, 0), c.x.at[4, :, lo], c.x.at[6, :, lo], c.plus)
        send(c, (PARTNER, DOWNWARD, 0), c.x.at[4, :, lo], c.x.at[5, :, lo], c.minus)

    def partner_hi(c):
        arrived(c, (OWN, SIDE, 1), c.x.at[4, :, hi])
        send(c, (PARTNER, DOWNWARD, 1), c.x.at[4, :, hi], c.x.at[5, :, hi], c.minus)
        send(c, (PARTNER, UPWARD, 1), c.x.at[4, :, hi], c.x.at[6, :, hi], c.plus)

    def partner_forward_up(c):
        arrived(c, (PARTNER, UPWARD, 0), c.x.at[6, :, lo])
        send(c, (PARTNER_AHEAD,), c.x.at[6, :, lo], c.x.at[7, :, lo], c.plus)

    def partner_forward_down(c):
        arrived(c, (PARTNER, DOWNWARD, 1), c.x.at[5, :, hi])
        send(c, (PARTNER_AHEAD,), c.x.at[5, :, hi], c.x.at[7, :, hi], c.minus)

    needs = {1: ((OWN, DOWNWARD, 0), lo), 2: ((OWN, UPWARD, 1), hi), 3: ((AHEAD,), None),
             5: ((PARTNER, DOWNWARD, 0), lo), 6: ((PARTNER, UPWARD, 1), hi), 7: ((PARTNER_AHEAD,), None)}
    begun = set()

    def multiply(c, j):
        if c.at not in begun:
            begun.add(c.at)
            for copy in (local[0], local[2]) if c is g else (local[1], local[3]):
                copy.wait()
            arrived(c, (BASIS,), c.w.at[hi])
        if j == 0 and c is a:
            arrived(c, (SWAP,), c.x.at[0, :, hi])
        if j in needs:
            name, cols = needs[j]
            arrived(c, name, c.x.at[j] if cols is None else c.x.at[j, :, cols])

        @pl.loop(0, WIDE // TILE)
        def _(n):
            cols = pl.ds(pl.multiple_of(n * TILE, TILE), TILE)
            c.p[j, :, cols] = jnp.dot(c.x[j], c.w[:, cols], preferred_element_type=F32)

        if j in ASIDE:
            for d in range(4):
                c.s1[j, d // 2, (first, second)[d % 2]] = encode(c.p[j, piece(c.q(d, 1))])
            send(c, (FIRST, j), c.s1.at[j], c.r1.at[j], c.sum_partner)
            return
        c.s1[j, UPWARD, first] = encode(c.p[j, piece(c.q(2, 0))])
        c.s1[j, UPWARD, second] = encode(c.p[j, piece(c.q(1, 1))])
        send(c, (FIRST, j), c.s1.at[j, UPWARD], c.r1.at[j, UPWARD], c.sum_plus)
        c.s1[j, DOWNWARD, first] = encode(c.p[j, piece(c.q(2, 1))])
        c.s1[j, DOWNWARD, second] = encode(c.p[j, piece(c.q(3, 0))])
        send(c, (FIRST, j), c.s1.at[j, DOWNWARD], c.r1.at[j, DOWNWARD], c.sum_minus)

    def sum_second(c, j):
        arrived(c, (FIRST, j), c.r1.at[j])
        if j in ASIDE:
            for d in range(4):
                at = piece(c.q(d, 0))
                c.p[j, at] = c.p[j, at] + decode(c.r1[j, d // 2, (first, second)[d % 2]])
            at = piece(c.q(2, 0))
            c.s2[j, UPWARD, :, lo] = encode(c.p[j, at, lo])
            c.s2[j, DOWNWARD, :, hi] = encode(c.p[j, at, hi])
            send(c, (SECOND, j), c.s2.at[j, UPWARD, :, lo], c.r2.at[j, UPWARD, :, lo], c.sum_plus)
            send(c, (SECOND, j), c.s2.at[j, DOWNWARD, :, hi], c.r2.at[j, DOWNWARD, :, hi], c.sum_minus)
            return
        c.s2[j, UPWARD] = encode(c.p[j, piece(c.q(1, 0))] + decode(c.r1[j, UPWARD, first]))
        send(c, (SECOND, j), c.s2.at[j, UPWARD], c.r2.at[j, UPWARD], c.sum_plus)
        c.s2[j, DOWNWARD] = encode(c.p[j, piece(c.q(3, 1))] + decode(c.r1[j, DOWNWARD, first]))
        send(c, (SECOND, j), c.s2.at[j, DOWNWARD], c.r2.at[j, DOWNWARD], c.sum_minus)

    def sum_partner(c, j):
        if j in ASIDE:
            arrived(c, (SECOND, j), c.r2.at[j, UPWARD])
            k = ASIDE.index(j)
            up, down = piece(c.q(1, 0)), piece(c.q(3, 0))
            c.s4[k, UPWARD, :, lo] = encode(c.p[j, up, lo] + decode(c.r2[j, UPWARD, :, lo]))
            c.s4[k, UPWARD, :, hi] = encode(c.p[j, up, hi])
            send(c, (THIRD, j), c.s4.at[k, UPWARD], c.r4.at[k, UPWARD], c.sum_plus)
            c.s4[k, DOWNWARD, :, lo] = encode(c.p[j, down, lo])
            c.s4[k, DOWNWARD, :, hi] = encode(c.p[j, down, hi] + decode(c.r2[j, DOWNWARD, :, hi]))
            send(c, (THIRD, j), c.s4.at[k, DOWNWARD], c.r4.at[k, DOWNWARD], c.sum_minus)
            return
        arrived(c, (SECOND, j), c.r2.at[j])
        c.s3[j] = encode(c.p[j, piece(c.q(0, 1))] + decode(c.r1[j, UPWARD, second]) + decode(c.r2[j, DOWNWARD]))
        send(c, (THIRD, j), c.s3.at[j], c.r3.at[j], c.sum_partner)
        at = piece(c.q(0, 0))
        c.p[j, at] = c.p[j, at] + decode(c.r1[j, DOWNWARD, second]) + decode(c.r2[j, UPWARD])

    def finish(c, j):
        at = piece(c.q(0, 0))
        if j in ASIDE:
            k = ASIDE.index(j)
            arrived(c, (THIRD, j), c.r4.at[k])
            c.rot[j, at] = (c.p[j, at] + decode(c.r4[k, UPWARD]) + decode(c.r4[k, DOWNWARD])).astype(BF16)
        else:
            arrived(c, (THIRD, j), c.r3.at[j])
            c.rot[j, at] = (c.p[j, at] + decode(c.r3[j])).astype(BF16)
        ref = c.rot.at[j, at]
        if j in DIRECT:
            send(c, (DONE, SIDE, j), ref, ref, c.sum_partner)
            for to in (c.sum_plus, c.sum_minus, c.sum_two):
                send(c, (DONE, j), ref, ref, to)
        else:
            send(c, (DONE, j), ref, ref, c.sum_plus)
            send(c, (DONE, j), ref, ref, c.sum_minus)
            send(c, (DONE, SIDE, j), ref, ref, c.sum_partner)

    def spread(c, j):
        arrived(c, (DONE, j), c.rot.at[j, pl.ds(0, 2 * PIECE)])
        ref = c.rot.at[j, piece(c.q(3, 0)), lo]
        send(c, (HALVES, j), ref, ref, c.sum_plus)
        ref = c.rot.at[j, piece(c.q(1, 0)), hi]
        send(c, (HALVES, j), ref, ref, c.sum_minus)
        if j in LATER:
            for d in (3, 1):
                ref = c.rot.at[j, piece(c.q(d, 0))]
                send(c, (DONE, SIDE, j), ref, ref, c.sum_partner)

    def across(c, j):
        if j in LATER:
            arrived(c, (HALVES, j), c.rot.at[j, first])
            ref = c.rot.at[j, piece(c.q(2, 0))]
            send(c, (DONE, SIDE, j), ref, ref, c.sum_partner)
            return
        arrived(c, (DONE, SIDE, j), c.rot.at[j, first])
        ref = c.rot.at[j, piece(c.q(0, 1))]
        if j in DIRECT:
            for to in (c.sum_two, c.sum_plus, c.sum_minus):
                send(c, (HALVES, j), ref, ref, to)
        else:
            send(c, (ACROSS, j), ref, ref, c.sum_plus)
            send(c, (ACROSS, j), ref, ref, c.sum_minus)

    def spread_across(c, j):
        arrived(c, (ACROSS, j), c.rot.at[j, pl.ds(0, 2 * PIECE)])
        ref = c.rot.at[j, piece(c.q(3, 1)), lo]
        send(c, (HALVES, j), ref, ref, c.sum_plus)
        ref = c.rot.at[j, piece(c.q(1, 1)), hi]
        send(c, (HALVES, j), ref, ref, c.sum_minus)

    def share_rows(c, j, rows):
        if c is a:
            send(c, (SHARED, j), rot_a.at[j, rows], rot_ao.at[j, rows], other)
        else:
            send(c, (SHARED, j), rot_g.at[j, rows, hi], rot_go.at[j, rows], other)

    def share_early(c, j):
        arrived(c, (DONE, j), c.rot.at[j, pl.ds(0, 3 * PIECE)])
        for d in range(4):
            share_rows(c, j, piece(c.q(d, 0)))

    def share(c, j):
        if j in DIRECT:
            arrived(c, (HALVES, j), c.rot.at[j, pl.ds(0, 3 * PIECE)])
            for d in range(4):
                share_rows(c, j, piece(c.q(d, 1)))
            return
        if j in LATER:
            arrived(c, (DONE, SIDE, j), c.rot.at[j, pl.ds(0, 4 * PIECE)])
        else:
            arrived(c, (HALVES, j), c.rot.at[j, pl.ds(0, 2 * PIECE)])
        share_rows(c, j, pl.ds(0, HALF))

    def receive(c, j):
        arrived(c, (SHARED, j), rot_ao.at[j] if c is a else rot_go.at[j])

    def ring_slot(up):
        return up + (up // 2) * (1 - 2 * (up % 2))

    def a_slot(t):
        return ring_slot((t % 4 + 4 - x) % 4) + 4 * ((t // 4 + yh) % 2)

    def g_slot(t):
        return ring_slot((t // 2 + 4 - z) % 4) + 4 * ((t + yl) % 2)

    def correlate(above, upto):
        @pl.loop(0, SLOTS)
        def _(t):
            last = jnp.maximum(a_slot(t), g_slot(t))

            @pl.when((last > above) & (last <= upto))
            def _():
                rows = jnp.concatenate([rot_g[g_slot(t), :, lo], rot_go[g_slot(t)]], axis=0)
                columns = jnp.concatenate([rot_a[a_slot(t)], rot_ao[a_slot(t)]], axis=0)
                sums[t // 4] += lax.dot_general(
                    rows, columns, (((0,), (0,)), ((), ())), preferred_element_type=F32)

    steps = (own, forward_up, forward_down, partner_lo, partner_hi, partner_forward_up, partner_forward_down,
             multiply, sum_second, sum_partner, finish, spread, across, spread_across, share, receive, share_early)
    for code in ORDER:
        c, step, j = (g, a)[code // 1000], code % 1000 // 10, code % 10
        if step < 7:
            steps[step](c)
        elif step < len(steps):
            steps[step](c, j)
        else:
            correlate(*PASSES[j])

    @pl.loop(0, NARROW // 64)
    def _(n):
        rows = pl.ds(pl.multiple_of(n * 64, 64), 64)
        out[rows] = (sums[0, rows] * sums[0, rows] + sums[1, rows] * sums[1, rows]) * (1.0 / TOKENS)

    assert len(names) == ARRIVALS
    pltpu.make_async_copy(total, total, send_sem).wait()


def on_device(acts, grads, qa, qs):
    vm = pltpu.VMEM
    sums = [vm((SLOTS, 2, 2 * PIECE, WIDE), BF16)] * 2 + [vm((SLOTS, 2, PIECE, WIDE), BF16)] * 2
    sums += [vm((SLOTS, PIECE, WIDE), BF16)] * 2 + [vm((max(len(ASIDE), 1), 2, PIECE, WIDE), BF16)] * 2
    args = [pltpu.with_memory_space_constraint(v, pltpu.HBM) for v in (acts, grads, qa, qs)]
    correction, _ = pl.pallas_call(
        kernel,
        out_shape=(jax.ShapeDtypeStruct((NARROW, WIDE), F32), pltpu.HBM((SENT, WIDE), BF16)),
        in_specs=[pl.BlockSpec(memory_space=pl.ANY)] * 4,
        out_specs=(pl.BlockSpec(memory_space=pltpu.VMEM), pl.BlockSpec(memory_space=pltpu.HBM)),
        scratch_shapes=[
            vm((SEQS, NARROW, WIDE), F32),
            vm((SLOTS, HALF, WIDE), BF16), vm((SLOTS, HALF, WIDE), BF16),
            vm((WIDE, WIDE), BF16), vm((WIDE, WIDE), BF16),
            vm((SLOTS, HALF, WIDE), F32), vm((SLOTS, HALF, WIDE), F32),
            vm((SLOTS, HALF, WIDE), BF16), vm((SLOTS, HALF, WIDE), BF16),
            vm((SLOTS, HALF, WIDE), BF16), vm((SLOTS, HALF, NARROW), BF16),
            *sums, *sums,
            pltpu.SemaphoreType.DMA((4,)),
            pltpu.SemaphoreType.DMA, pltpu.SemaphoreType.DMA((ARRIVALS,)),
        ],
        compiler_params=pltpu.CompilerParams(
            collective_id=0, has_side_effects=True, vmem_limit_bytes=48 * 2 ** 20),
        cost_estimate=pl.CostEstimate(flops=6442450944, bytes_accessed=5 * 2 ** 20, transcendentals=0),
        name="rotate_and_correlate",
    )(*args)
    return correction


def solution(mesh):
    return jax.shard_map(
        on_device,
        mesh=mesh,
        in_specs=(P("row", "col"), P("col", "row"), P("col", "row"), P("row", "col")),
        out_specs=P("col", "row"),
        check_vma=False,
    )
```

```python
import jax
import jax.numpy as jnp
from jax import lax
from jax.experimental import pallas as pl
from jax.experimental.pallas import tpu as pltpu
from jax.sharding import PartitionSpec as P

MESH = pl.DeviceIdType.MESH
F32, BF16 = jnp.float32, jnp.bfloat16

TOKENS, D, SEQS = 2048, 8192, 2
SLOTS = 8
HALF = TOKENS // SLOTS // 2
PIECE = HALF // SLOTS
WIDE = 1024
NARROW = WIDE // 2
TILE = 512
LAST_TILE = 512
DIRECT = (6, 7)
ASIDE = (2, 3)
LATER = (3,)
ARRIVALS = 138
SENT = 8000

PASSES = ((-1, 0), (0, 2), (2, 4), (4, 6))

UP = 2.0 ** 30

ORDER = (
    0, 1000, 1070, 70, 20, 1020, 1010, 30, 1071, 71, 10, 72, 40, 80, 1030, 1072, 74, 1040, 1074, 1073, 1081, 1080, 81,
    73, 50, 60, 75, 1084, 84, 1050, 90, 82, 1060, 1082, 1090, 1083, 1091, 1075, 91, 1076, 85, 94, 77, 1094, 83, 1100,
    76, 1093, 1092, 1101, 100, 95, 101, 1085, 92, 1077, 1086, 104, 1104, 1102, 1103, 93, 86, 87, 1095, 105, 1121, 121,
    102, 1087, 1096, 1120, 1122, 103, 124, 96, 111, 1124, 120, 1105, 1111, 110, 1112, 97, 1131, 125, 131, 1106, 1097,
    122, 1132, 1110, 113, 106, 130, 1113, 1114, 1130, 1125, 1134, 112, 1126, 107, 132, 134, 114, 141, 115, 1107, 135,
    1142, 123, 1123, 1140, 1141, 1135, 126, 1166, 140, 1115, 1144, 1146, 127, 1127, 142, 144, 143, 1143, 145, 170,
    1145, 171, 166, 146, 167, 1167, 172, 1147, 147, 173,
)


def encode(v):
    v = v * UP
    return (v * v * v).astype(BF16)


def decode(c):
    c = c.astype(F32)
    size = jnp.maximum(jnp.abs(c), 2.0 ** -126)
    return c * (jnp.exp2(jnp.log2(size) * (-2.0 / 3.0)) * (1.0 / UP))


class Chain:
    def __init__(self, **refs):
        self.__dict__.update(refs)


def kernel(acts, grads, qa, qs, out, total,
           sums, xa, xg, wa, wg, pa, pg, rot_a, rot_g, rot_ao, rot_go,
           s1a, r1a, s2a, r2a, s3a, r3a, s4a, r4a, s1g, r1g, s2g, r2g, s3g, r3g, s4g, r4g,
           local_sem, send_sem, recv_sem):
    row, col = lax.axis_index("row"), lax.axis_index("col")
    yh, x = row // 4, row % 4
    z, yl, h = col // 4, (col // 2) % 2, col % 2

    def dev(dyh, dx, dz, dyl, core):
        return ((yh + dyh) % 2 * 4 + (x + dx) % 4, (z + dz) % 4 * 4 + (yl + dyl) % 2 * 2 + core)

    x_plus, x_minus = dev(0, 1, 0, 0, h), dev(0, 3, 0, 0, h)
    z_plus, z_minus = dev(0, 0, 1, 0, h), dev(0, 0, 3, 0, h)
    y_far, y_near = dev(1, 0, 0, 0, h), dev(0, 0, 0, 1, h)
    other = dev(0, 0, 0, 0, 1 - h)
    x_plus_o, x_minus_o, y_far_o = dev(0, 1, 0, 0, 1 - h), dev(0, 3, 0, 0, 1 - h), dev(1, 0, 0, 0, 1 - h)

    barrier = pltpu.get_barrier_semaphore()
    x_two, z_two = dev(0, 2, 0, 0, h), dev(0, 0, 2, 0, h)
    neighbours = (x_plus, x_minus, z_plus, z_minus, y_far, y_near, other, x_plus_o, x_minus_o, y_far_o, x_two, z_two)
    for n in neighbours:
        pl.semaphore_signal(barrier, inc=1, device_id=n, device_id_type=MESH)

    names = {}

    def arrival(c, name):
        return recv_sem.at[names.setdefault((c.at,) + name, len(names))]

    def send(c, name, src, dst, to):
        pltpu.make_async_remote_copy(
            src_ref=src, dst_ref=dst, send_sem=send_sem, recv_sem=arrival(c, name),
            device_id=to, device_id_type=MESH).start()

    def arrived(c, name, ref):
        pltpu.make_async_remote_copy(
            src_ref=ref, dst_ref=ref, send_sem=send_sem, recv_sem=arrival(c, name),
            device_id=other, device_id_type=MESH).wait_recv()

    def piece(q):
        return pl.ds(pl.multiple_of(q * PIECE, PIECE), PIECE)

    lo, hi = pl.ds(0, NARROW), pl.ds(NARROW, NARROW)
    mine = pl.ds(pl.multiple_of(h * HALF, HALF), HALF)
    its = pl.ds(pl.multiple_of((1 - h) * HALF, HALF), HALF)
    first, second = pl.ds(0, PIECE), pl.ds(PIECE, PIECE)

    a = Chain(at=1, plus=x_plus, minus=x_minus, partner=y_far,
              sum_plus=z_plus, sum_minus=z_minus, sum_two=z_two, sum_partner=y_near,
              plus_o=x_plus_o, minus_o=x_minus_o, partner_o=y_far_o,
              own_lo=acts.at[mine], own_hi=acts.at[its],
              q=lambda d, e: ((z + d) % 4) * 2 + (yl + e) % 2,
              x=xa, w=wa, p=pa, rot=rot_a, s1=s1a, r1=r1a, s2=s2a, r2=r2a, s3=s3a, r3=r3a,
              s4=s4a, r4=r4a)
    g = Chain(at=0, plus=z_plus, minus=z_minus, partner=y_near,
              sum_plus=x_plus, sum_minus=x_minus, sum_two=x_two, sum_partner=y_far,
              plus_o=z_plus, minus_o=z_minus, partner_o=y_near,
              own_lo=grads.at[:, lo], own_hi=grads.at[:, hi],
              q=lambda d, e: ((yh + e) % 2) * 4 + (x + d) % 4,
              x=xg, w=wg, p=pg, rot=rot_g, s1=s1g, r1=r1g, s2=s2g, r2=r2g, s3=s3g, r3=r3g,
              s4=s4g, r4=r4g)

    local = [
        pltpu.make_async_copy(grads, xg.at[0], local_sem.at[0]),
        pltpu.make_async_copy(acts.at[mine], xa.at[0, :, lo], local_sem.at[1]),
        pltpu.make_async_copy(qs, wg.at[:, lo], local_sem.at[2]),
        pltpu.make_async_copy(qa, wa.at[lo], local_sem.at[3]),
    ]
    for copy in local:
        copy.start()

    pl.semaphore_wait(barrier, len(neighbours))

    UPWARD, DOWNWARD, SIDE = 0, 1, 2
    OWN, AHEAD, PARTNER, PARTNER_AHEAD, SWAP, BASIS, FIRST, SECOND, THIRD, DONE, ACROSS, HALVES, SHARED = range(13)

    def own(c):
        send(c, (OWN, UPWARD, 0), c.own_lo, c.x.at[2, :, lo], c.plus)
        send(c, (OWN, DOWNWARD, 1), c.own_hi, c.x.at[1, :, hi], c.minus_o)
        send(c, (OWN, SIDE, 0), c.own_lo, c.x.at[4, :, lo], c.partner)
        send(c, (OWN, UPWARD, 1), c.own_hi, c.x.at[2, :, hi], c.plus_o)
        send(c, (OWN, DOWNWARD, 0), c.own_lo, c.x.at[1, :, lo], c.minus)
        send(c, (OWN, SIDE, 1), c.own_hi, c.x.at[4, :, hi], c.partner_o)
        if c is a:
            send(c, (SWAP,), acts.at[its], xa.at[0, :, hi], other)
            send(c, (BASIS,), qa, wa.at[hi], other)
            sums[...] = jnp.zeros_like(sums)
        else:
            send(c, (BASIS,), qs, wg.at[:, hi], other)

    def forward_up(c):
        arrived(c, (OWN, UPWARD, 0), c.x.at[2, :, lo])
        send(c, (AHEAD,), c.x.at[2, :, lo], c.x.at[3, :, lo], c.plus)

    def forward_down(c):
        arrived(c, (OWN, DOWNWARD, 1), c.x.at[1, :, hi])
        send(c, (AHEAD,), c.x.at[1, :, hi], c.x.at[3, :, hi], c.minus)

    def partner_lo(c):
        arrived(c, (OWN, SIDE, 0), c.x.at[4, :, lo])
        send(c, (PARTNER, UPWARD, 0), c.x.at[4, :, lo], c.x.at[6, :, lo], c.plus)
        send(c, (PARTNER, DOWNWARD, 0), c.x.at[4, :, lo], c.x.at[5, :, lo], c.minus)

    def partner_hi(c):
        arrived(c, (OWN, SIDE, 1), c.x.at[4, :, hi])
        send(c, (PARTNER, DOWNWARD, 1), c.x.at[4, :, hi], c.x.at[5, :, hi], c.minus)
        send(c, (PARTNER, UPWARD, 1), c.x.at[4, :, hi], c.x.at[6, :, hi], c.plus)

    def partner_forward_up(c):
        arrived(c, (PARTNER, UPWARD, 0), c.x.at[6, :, lo])
        send(c, (PARTNER_AHEAD,), c.x.at[6, :, lo], c.x.at[7, :, lo], c.plus)

    def partner_forward_down(c):
        arrived(c, (PARTNER, DOWNWARD, 1), c.x.at[5, :, hi])
        send(c, (PARTNER_AHEAD,), c.x.at[5, :, hi], c.x.at[7, :, hi], c.minus)

    needs = {1: ((OWN, DOWNWARD, 0), lo), 2: ((OWN, UPWARD, 1), hi), 3: ((AHEAD,), None),
             5: ((PARTNER, DOWNWARD, 0), lo), 6: ((PARTNER, UPWARD, 1), hi), 7: ((PARTNER_AHEAD,), None)}
    begun = set()

    def multiply(c, j):
        if c.at not in begun:
            begun.add(c.at)
            for copy in (local[0], local[2]) if c is g else (local[1], local[3]):
                copy.wait()
            arrived(c, (BASIS,), c.w.at[hi])
        if j == 0 and c is a:
            arrived(c, (SWAP,), c.x.at[0, :, hi])
        if j in needs:
            name, cols = needs[j]
            arrived(c, name, c.x.at[j] if cols is None else c.x.at[j, :, cols])

        @pl.loop(0, WIDE // TILE)
        def _(n):
            cols = pl.ds(pl.multiple_of(n * TILE, TILE), TILE)
            c.p[j, :, cols] = jnp.dot(c.x[j], c.w[:, cols], preferred_element_type=F32)

        if j in ASIDE:
            for d in range(4):
                c.s1[j, d // 2, (first, second)[d % 2]] = encode(c.p[j, piece(c.q(d, 1))])
            send(c, (FIRST, j), c.s1.at[j], c.r1.at[j], c.sum_partner)
            return
        c.s1[j, UPWARD, first] = encode(c.p[j, piece(c.q(2, 0))])
        c.s1[j, UPWARD, second] = encode(c.p[j, piece(c.q(1, 1))])
        send(c, (FIRST, j), c.s1.at[j, UPWARD], c.r1.at[j, UPWARD], c.sum_plus)
        c.s1[j, DOWNWARD, first] = encode(c.p[j, piece(c.q(2, 1))])
        c.s1[j, DOWNWARD, second] = encode(c.p[j, piece(c.q(3, 0))])
        send(c, (FIRST, j), c.s1.at[j, DOWNWARD], c.r1.at[j, DOWNWARD], c.sum_minus)

    def sum_second(c, j):
        arrived(c, (FIRST, j), c.r1.at[j])
        if j in ASIDE:
            for d in range(4):
                at = piece(c.q(d, 0))
                c.p[j, at] = c.p[j, at] + decode(c.r1[j, d // 2, (first, second)[d % 2]])
            at = piece(c.q(2, 0))
            c.s2[j, UPWARD, :, lo] = encode(c.p[j, at, lo])
            c.s2[j, DOWNWARD, :, hi] = encode(c.p[j, at, hi])
            send(c, (SECOND, j), c.s2.at[j, UPWARD, :, lo], c.r2.at[j, UPWARD, :, lo], c.sum_plus)
            send(c, (SECOND, j), c.s2.at[j, DOWNWARD, :, hi], c.r2.at[j, DOWNWARD, :, hi], c.sum_minus)
            return
        c.s2[j, UPWARD] = encode(c.p[j, piece(c.q(1, 0))] + decode(c.r1[j, UPWARD, first]))
        send(c, (SECOND, j), c.s2.at[j, UPWARD], c.r2.at[j, UPWARD], c.sum_plus)
        c.s2[j, DOWNWARD] = encode(c.p[j, piece(c.q(3, 1))] + decode(c.r1[j, DOWNWARD, first]))
        send(c, (SECOND, j), c.s2.at[j, DOWNWARD], c.r2.at[j, DOWNWARD], c.sum_minus)

    def sum_partner(c, j):
        if j in ASIDE:
            arrived(c, (SECOND, j), c.r2.at[j, UPWARD])
            k = ASIDE.index(j)
            up, down = piece(c.q(1, 0)), piece(c.q(3, 0))
            c.s4[k, UPWARD, :, lo] = encode(c.p[j, up, lo] + decode(c.r2[j, UPWARD, :, lo]))
            c.s4[k, UPWARD, :, hi] = encode(c.p[j, up, hi])
            send(c, (THIRD, j), c.s4.at[k, UPWARD], c.r4.at[k, UPWARD], c.sum_plus)
            c.s4[k, DOWNWARD, :, lo] = encode(c.p[j, down, lo])
            c.s4[k, DOWNWARD, :, hi] = encode(c.p[j, down, hi] + decode(c.r2[j, DOWNWARD, :, hi]))
            send(c, (THIRD, j), c.s4.at[k, DOWNWARD], c.r4.at[k, DOWNWARD], c.sum_minus)
            return
        arrived(c, (SECOND, j), c.r2.at[j])
        c.s3[j] = encode(c.p[j, piece(c.q(0, 1))] + decode(c.r1[j, UPWARD, second]) + decode(c.r2[j, DOWNWARD]))
        send(c, (THIRD, j), c.s3.at[j], c.r3.at[j], c.sum_partner)
        at = piece(c.q(0, 0))
        c.p[j, at] = c.p[j, at] + decode(c.r1[j, DOWNWARD, second]) + decode(c.r2[j, UPWARD])

    def finish(c, j):
        at = piece(c.q(0, 0))
        if j in ASIDE:
            k = ASIDE.index(j)
            arrived(c, (THIRD, j), c.r4.at[k])
            c.rot[j, at] = (c.p[j, at] + decode(c.r4[k, UPWARD]) + decode(c.r4[k, DOWNWARD])).astype(BF16)
        else:
            arrived(c, (THIRD, j), c.r3.at[j])
            c.rot[j, at] = (c.p[j, at] + decode(c.r3[j])).astype(BF16)
        ref = c.rot.at[j, at]
        if j in DIRECT:
            send(c, (DONE, SIDE, j), ref, ref, c.sum_partner)
            for to in (c.sum_plus, c.sum_minus, c.sum_two):
                send(c, (DONE, j), ref, ref, to)
        else:
            send(c, (DONE, j), ref, ref, c.sum_plus)
            send(c, (DONE, j), ref, ref, c.sum_minus)
            send(c, (DONE, SIDE, j), ref, ref, c.sum_partner)

    def spread(c, j):
        arrived(c, (DONE, j), c.rot.at[j, pl.ds(0, 2 * PIECE)])
        ref = c.rot.at[j, piece(c.q(3, 0)), lo]
        send(c, (HALVES, j), ref, ref, c.sum_plus)
        ref = c.rot.at[j, piece(c.q(1, 0)), hi]
        send(c, (HALVES, j), ref, ref, c.sum_minus)
        if j in LATER:
            for d in (3, 1):
                ref = c.rot.at[j, piece(c.q(d, 0))]
                send(c, (DONE, SIDE, j), ref, ref, c.sum_partner)

    def across(c, j):
        if j in LATER:
            arrived(c, (HALVES, j), c.rot.at[j, first])
            ref = c.rot.at[j, piece(c.q(2, 0))]
            send(c, (DONE, SIDE, j), ref, ref, c.sum_partner)
            return
        arrived(c, (DONE, SIDE, j), c.rot.at[j, first])
        ref = c.rot.at[j, piece(c.q(0, 1))]
        if j in DIRECT:
            for to in (c.sum_two, c.sum_plus, c.sum_minus):
                send(c, (HALVES, j), ref, ref, to)
        else:
            send(c, (ACROSS, j), ref, ref, c.sum_plus)
            send(c, (ACROSS, j), ref, ref, c.sum_minus)

    def spread_across(c, j):
        arrived(c, (ACROSS, j), c.rot.at[j, pl.ds(0, 2 * PIECE)])
        ref = c.rot.at[j, piece(c.q(3, 1)), lo]
        send(c, (HALVES, j), ref, ref, c.sum_plus)
        ref = c.rot.at[j, piece(c.q(1, 1)), hi]
        send(c, (HALVES, j), ref, ref, c.sum_minus)

    def share_rows(c, j, rows):
        now = sum(j > upto for _, upto in PASSES)
        if c is a:
            send(g, (SHARED, now), rot_a.at[j, rows], rot_ao.at[j, rows], other)
        else:
            send(g, (SHARED, now), rot_g.at[j, rows, hi], rot_go.at[j, rows], other)

    def share_early(c, j):
        arrived(c, (DONE, j), c.rot.at[j, pl.ds(0, 3 * PIECE)])
        for d in range(4):
            share_rows(c, j, piece(c.q(d, 0)))

    def share(c, j):
        if j in DIRECT:
            arrived(c, (HALVES, j), c.rot.at[j, pl.ds(0, 3 * PIECE)])
            for d in range(4):
                share_rows(c, j, piece(c.q(d, 1)))
            return
        if j in LATER:
            arrived(c, (DONE, SIDE, j), c.rot.at[j, pl.ds(0, 4 * PIECE)])
        else:
            arrived(c, (HALVES, j), c.rot.at[j, pl.ds(0, 2 * PIECE)])
        share_rows(c, j, pl.ds(0, HALF))

    def receive(now):
        above, upto = (PASSES + ((SLOTS - 2, SLOTS - 1),))[now]
        arrived(g, (SHARED, now), wa.at[pl.ds(0, (upto - above) * (HALF + HALF // 2))])

    def ring_slot(up):
        return up + (up // 2) * (1 - 2 * (up % 2))

    def a_slot(t):
        return ring_slot((t % 4 + 4 - x) % 4) + 4 * ((t // 4 + yh) % 2)

    def g_slot(t):
        return ring_slot((t // 2 + 4 - z) % 4) + 4 * ((t + yl) % 2)

    def correlate(above, upto):
        @pl.loop(0, SLOTS)
        def _(t):
            last = jnp.maximum(a_slot(t), g_slot(t))

            @pl.when((last > above) & (last <= upto))
            def _():
                rows = jnp.concatenate([rot_g[g_slot(t), :, lo], rot_go[g_slot(t)]], axis=0)
                columns = jnp.concatenate([rot_a[a_slot(t)], rot_ao[a_slot(t)]], axis=0)
                sums[t // 4] += lax.dot_general(
                    rows, columns, (((0,), (0,)), ((), ())), preferred_element_type=F32)

    steps = (own, forward_up, forward_down, partner_lo, partner_hi, partner_forward_up, partner_forward_down,
             multiply, sum_second, sum_partner, finish, spread, across, spread_across, share, None, share_early)
    for code in ORDER:
        c, step, j = (g, a)[code // 1000], code % 1000 // 10, code % 10
        if step < 7:
            steps[step](c)
        elif step < len(steps):
            steps[step](c, j)
        else:
            receive(j)
            correlate(*PASSES[j])

    receive(len(PASSES))
    last_a = (yh + 1) % 2 * 4 + (x + 2) % 4
    last_g = (z + 2) % 4 * 2 + (yl + 1) % 2
    distinct = jnp.where(last_a == last_g, 0.0, 1.0)
    in_first_a = jnp.where(last_a < 4, 1.0, 0.0)
    in_first_g = jnp.where(last_g < 4, distinct, 0.0)

    @pl.loop(0, WIDE // LAST_TILE)
    def _(n):
        cols = pl.ds(pl.multiple_of(n * LAST_TILE, LAST_TILE), LAST_TILE)

        def product(t):
            rows = jnp.concatenate([rot_g[g_slot(t), :, lo], rot_go[g_slot(t)]], axis=0)
            columns = jnp.concatenate([rot_a[a_slot(t), :, cols], rot_ao[a_slot(t), :, cols]], axis=0)
            return lax.dot_general(rows, columns, (((0,), (0,)), ((), ())), preferred_element_type=F32)

        for_a, for_g = product(last_a), product(last_g)
        block0 = sums[0, :, cols] + for_a * in_first_a + for_g * in_first_g
        block1 = sums[1, :, cols] + for_a * (1.0 - in_first_a) + for_g * (distinct - in_first_g)
        out[:, cols] = (block0 * block0 + block1 * block1) * (1.0 / TOKENS)

    assert len(names) == ARRIVALS
    pltpu.make_async_copy(total, total, send_sem).wait()


def on_device(acts, grads, qa, qs):
    vm = pltpu.VMEM
    sums = [vm((SLOTS, 2, 2 * PIECE, WIDE), BF16)] * 2 + [vm((SLOTS, 2, PIECE, WIDE), BF16)] * 2
    sums += [vm((SLOTS, PIECE, WIDE), BF16)] * 2 + [vm((max(len(ASIDE), 1), 2, PIECE, WIDE), BF16)] * 2
    args = [pltpu.with_memory_space_constraint(v, pltpu.HBM) for v in (acts, grads, qa, qs)]
    correction, _ = pl.pallas_call(
        kernel,
        out_shape=(jax.ShapeDtypeStruct((NARROW, WIDE), F32), pltpu.HBM((SENT, WIDE), BF16)),
        in_specs=[pl.BlockSpec(memory_space=pl.ANY)] * 4,
        out_specs=(pl.BlockSpec(memory_space=pltpu.VMEM), pl.BlockSpec(memory_space=pltpu.HBM)),
        scratch_shapes=[
            vm((SEQS, NARROW, WIDE), F32),
            vm((SLOTS, HALF, WIDE), BF16), vm((SLOTS, HALF, WIDE), BF16),
            vm((WIDE, WIDE), BF16), vm((WIDE, WIDE), BF16),
            vm((SLOTS, HALF, WIDE), F32), vm((SLOTS, HALF, WIDE), F32),
            vm((SLOTS, HALF, WIDE), BF16), vm((SLOTS, HALF, WIDE), BF16),
            vm((SLOTS, HALF, WIDE), BF16), vm((SLOTS, HALF, NARROW), BF16),
            *sums, *sums,
            pltpu.SemaphoreType.DMA((4,)),
            pltpu.SemaphoreType.DMA, pltpu.SemaphoreType.DMA((ARRIVALS,)),
        ],
        compiler_params=pltpu.CompilerParams(
            collective_id=0, has_side_effects=True, vmem_limit_bytes=48 * 2 ** 20),
        cost_estimate=pl.CostEstimate(flops=6442450944, bytes_accessed=5 * 2 ** 20, transcendentals=0),
        name="rotate_and_correlate",
    )(*args)
    return correction


def solution(mesh):
    return jax.shard_map(
        on_device,
        mesh=mesh,
        in_specs=(P("row", "col"), P("col", "row"), P("col", "row"), P("row", "col")),
        out_specs=P("col", "row"),
        check_vma=False,
    )
```

```python
import jax
import jax.numpy as jnp
from jax import lax
from jax.experimental import pallas as pl
from jax.experimental.pallas import tpu as pltpu
from jax.sharding import PartitionSpec as P

MESH = pl.DeviceIdType.MESH
F32, BF16 = jnp.float32, jnp.bfloat16

TOKENS, D, SEQS = 2048, 8192, 2
SLOTS = 8
HALF = TOKENS // SLOTS // 2
PIECE = HALF // SLOTS
WIDE = 1024
NARROW = WIDE // 2
TILE = 512
LAST_TILE = 512
DIRECT = (6, 7)
ASIDE = (1, 2)
LATER = (2,)
ARRIVALS = 138
SENT = 8000

PASSES = ((-1, 0), (0, 1), (1, 4), (4, 6))

UP = 2.0 ** 30

ORDER = (
    0, 1000, 70, 1070, 1010, 1020, 10, 20, 30, 40, 1071, 74, 72, 1030, 73, 1080, 71, 1040, 1074, 1073, 80, 1081, 60,
    84, 75, 50, 1090, 83, 1072, 1060, 1050, 1084, 90, 1083, 1076, 94, 1075, 1091, 1100, 81, 85, 93, 76, 1094, 1082,
    82, 1093, 77, 100, 1086, 104, 1120, 95, 1085, 1104, 1077, 1101, 91, 92, 1103, 86, 1092, 103, 1096, 1095, 105, 87,
    1121, 101, 1124, 124, 102, 1087, 110, 96, 123, 120, 1123, 1105, 113, 1114, 1102, 1106, 111, 1110, 97, 1097, 1134,
    121, 112, 106, 1111, 1130, 1113, 1112, 130, 134, 125, 1125, 1133, 1131, 131, 1126, 1115, 133, 107, 122, 1140,
    1166, 114, 1107, 1122, 166, 140, 126, 1141, 135, 1135, 115, 143, 141, 1144, 127, 1143, 1146, 1127, 142, 167, 144,
    1142, 170, 1145, 171, 146, 1167, 145, 172, 147, 1147, 173,
)


def encode(v):
    v = v * UP
    return (v * v * v).astype(BF16)


def decode(c):
    c = c.astype(F32)
    size = jnp.maximum(jnp.abs(c), 2.0 ** -126)
    return c * (jnp.exp2(jnp.log2(size) * (-2.0 / 3.0)) * (1.0 / UP))


class Chain:
    def __init__(self, **refs):
        self.__dict__.update(refs)


def kernel(acts, grads, qa, qs, out, total,
           sums, xa, xg, wa, wg, pa, pg, rot_a, rot_g, rot_ao, rot_go,
           s1a, r1a, s2a, r2a, s3a, r3a, s4a, r4a, s1g, r1g, s2g, r2g, s3g, r3g, s4g, r4g,
           local_sem, send_sem, recv_sem):
    row, col = lax.axis_index("row"), lax.axis_index("col")
    yh, x = row // 4, row % 4
    z, yl, h = col // 4, (col // 2) % 2, col % 2

    def dev(dyh, dx, dz, dyl, core):
        return ((yh + dyh) % 2 * 4 + (x + dx) % 4, (z + dz) % 4 * 4 + (yl + dyl) % 2 * 2 + core)

    x_plus, x_minus = dev(0, 1, 0, 0, h), dev(0, 3, 0, 0, h)
    z_plus, z_minus = dev(0, 0, 1, 0, h), dev(0, 0, 3, 0, h)
    y_far, y_near = dev(1, 0, 0, 0, h), dev(0, 0, 0, 1, h)
    other = dev(0, 0, 0, 0, 1 - h)
    x_plus_o, x_minus_o, y_far_o = dev(0, 1, 0, 0, 1 - h), dev(0, 3, 0, 0, 1 - h), dev(1, 0, 0, 0, 1 - h)

    barrier = pltpu.get_barrier_semaphore()
    x_two, z_two = dev(0, 2, 0, 0, h), dev(0, 0, 2, 0, h)
    neighbours = (x_plus, x_minus, z_plus, z_minus, y_far, y_near, other, x_plus_o, x_minus_o, y_far_o, x_two, z_two)
    for n in neighbours:
        pl.semaphore_signal(barrier, inc=1, device_id=n, device_id_type=MESH)

    names = {}

    def arrival(c, name):
        return recv_sem.at[names.setdefault((c.at,) + name, len(names))]

    def send(c, name, src, dst, to):
        pltpu.make_async_remote_copy(
            src_ref=src, dst_ref=dst, send_sem=send_sem, recv_sem=arrival(c, name),
            device_id=to, device_id_type=MESH).start()

    def arrived(c, name, ref):
        pltpu.make_async_remote_copy(
            src_ref=ref, dst_ref=ref, send_sem=send_sem, recv_sem=arrival(c, name),
            device_id=other, device_id_type=MESH).wait_recv()

    def piece(q):
        return pl.ds(pl.multiple_of(q * PIECE, PIECE), PIECE)

    lo, hi = pl.ds(0, NARROW), pl.ds(NARROW, NARROW)
    mine = pl.ds(pl.multiple_of(h * HALF, HALF), HALF)
    its = pl.ds(pl.multiple_of((1 - h) * HALF, HALF), HALF)
    first, second = pl.ds(0, PIECE), pl.ds(PIECE, PIECE)

    a = Chain(at=1, plus=x_plus, minus=x_minus, partner=y_far,
              sum_plus=z_plus, sum_minus=z_minus, sum_two=z_two, sum_partner=y_near,
              plus_o=x_plus_o, minus_o=x_minus_o, partner_o=y_far_o,
              own_lo=acts.at[mine], own_hi=acts.at[its],
              q=lambda d, e: ((z + d) % 4) * 2 + (yl + e) % 2,
              x=xa, w=wa, p=pa, rot=rot_a, s1=s1a, r1=r1a, s2=s2a, r2=r2a, s3=s3a, r3=r3a,
              s4=s4a, r4=r4a)
    g = Chain(at=0, plus=z_plus, minus=z_minus, partner=y_near,
              sum_plus=x_plus, sum_minus=x_minus, sum_two=x_two, sum_partner=y_far,
              plus_o=z_plus, minus_o=z_minus, partner_o=y_near,
              own_lo=grads.at[:, lo], own_hi=grads.at[:, hi],
              q=lambda d, e: ((yh + e) % 2) * 4 + (x + d) % 4,
              x=xg, w=wg, p=pg, rot=rot_g, s1=s1g, r1=r1g, s2=s2g, r2=r2g, s3=s3g, r3=r3g,
              s4=s4g, r4=r4g)

    local = [
        pltpu.make_async_copy(grads, xg.at[0], local_sem.at[0]),
        pltpu.make_async_copy(acts.at[mine], xa.at[0, :, lo], local_sem.at[1]),
        pltpu.make_async_copy(qs, wg.at[:, lo], local_sem.at[2]),
        pltpu.make_async_copy(qa, wa.at[lo], local_sem.at[3]),
    ]
    for copy in local:
        copy.start()

    pl.semaphore_wait(barrier, len(neighbours))

    UPWARD, DOWNWARD, SIDE = 0, 1, 2
    OWN, AHEAD, PARTNER, PARTNER_AHEAD, SWAP, BASIS, FIRST, SECOND, THIRD, DONE, ACROSS, HALVES, SHARED = range(13)

    def own(c):
        send(c, (OWN, UPWARD, 0), c.own_lo, c.x.at[2, :, lo], c.plus)
        send(c, (OWN, DOWNWARD, 1), c.own_hi, c.x.at[1, :, hi], c.minus_o)
        send(c, (OWN, SIDE, 0), c.own_lo, c.x.at[4, :, lo], c.partner)
        send(c, (OWN, UPWARD, 1), c.own_hi, c.x.at[2, :, hi], c.plus_o)
        send(c, (OWN, DOWNWARD, 0), c.own_lo, c.x.at[1, :, lo], c.minus)
        send(c, (OWN, SIDE, 1), c.own_hi, c.x.at[4, :, hi], c.partner_o)
        if c is a:
            send(c, (SWAP,), acts.at[its], xa.at[0, :, hi], other)
            send(c, (BASIS,), qa, wa.at[hi], other)
            sums[...] = jnp.zeros_like(sums)
        else:
            send(c, (BASIS,), qs, wg.at[:, hi], other)

    def forward_up(c):
        arrived(c, (OWN, UPWARD, 0), c.x.at[2, :, lo])
        send(c, (AHEAD,), c.x.at[2, :, lo], c.x.at[3, :, lo], c.plus)

    def forward_down(c):
        arrived(c, (OWN, DOWNWARD, 1), c.x.at[1, :, hi])
        send(c, (AHEAD,), c.x.at[1, :, hi], c.x.at[3, :, hi], c.minus)

    def partner_lo(c):
        arrived(c, (OWN, SIDE, 0), c.x.at[4, :, lo])
        send(c, (PARTNER, UPWARD, 0), c.x.at[4, :, lo], c.x.at[6, :, lo], c.plus)
        send(c, (PARTNER, DOWNWARD, 0), c.x.at[4, :, lo], c.x.at[5, :, lo], c.minus)

    def partner_hi(c):
        arrived(c, (OWN, SIDE, 1), c.x.at[4, :, hi])
        send(c, (PARTNER, DOWNWARD, 1), c.x.at[4, :, hi], c.x.at[5, :, hi], c.minus)
        send(c, (PARTNER, UPWARD, 1), c.x.at[4, :, hi], c.x.at[6, :, hi], c.plus)

    def partner_forward_up(c):
        arrived(c, (PARTNER, UPWARD, 0), c.x.at[6, :, lo])
        send(c, (PARTNER_AHEAD,), c.x.at[6, :, lo], c.x.at[7, :, lo], c.plus)

    def partner_forward_down(c):
        arrived(c, (PARTNER, DOWNWARD, 1), c.x.at[5, :, hi])
        send(c, (PARTNER_AHEAD,), c.x.at[5, :, hi], c.x.at[7, :, hi], c.minus)

    needs = {1: ((OWN, DOWNWARD, 0), lo), 2: ((OWN, UPWARD, 1), hi), 3: ((AHEAD,), None),
             5: ((PARTNER, DOWNWARD, 0), lo), 6: ((PARTNER, UPWARD, 1), hi), 7: ((PARTNER_AHEAD,), None)}
    begun = set()

    def multiply(c, j):
        if c.at not in begun:
            begun.add(c.at)
            for copy in (local[0], local[2]) if c is g else (local[1], local[3]):
                copy.wait()
            arrived(c, (BASIS,), c.w.at[hi])
        if j == 0 and c is a:
            arrived(c, (SWAP,), c.x.at[0, :, hi])
        if j in needs:
            name, cols = needs[j]
            arrived(c, name, c.x.at[j] if cols is None else c.x.at[j, :, cols])

        @pl.loop(0, WIDE // TILE)
        def _(n):
            cols = pl.ds(pl.multiple_of(n * TILE, TILE), TILE)
            c.p[j, :, cols] = jnp.dot(c.x[j], c.w[:, cols], preferred_element_type=F32)

        if j in ASIDE:
            for d in range(4):
                c.s1[j, d // 2, (first, second)[d % 2]] = encode(c.p[j, piece(c.q(d, 1))])
            send(c, (FIRST, j), c.s1.at[j], c.r1.at[j], c.sum_partner)
            return
        c.s1[j, UPWARD, first] = encode(c.p[j, piece(c.q(2, 0))])
        c.s1[j, UPWARD, second] = encode(c.p[j, piece(c.q(1, 1))])
        send(c, (FIRST, j), c.s1.at[j, UPWARD], c.r1.at[j, UPWARD], c.sum_plus)
        c.s1[j, DOWNWARD, first] = encode(c.p[j, piece(c.q(2, 1))])
        c.s1[j, DOWNWARD, second] = encode(c.p[j, piece(c.q(3, 0))])
        send(c, (FIRST, j), c.s1.at[j, DOWNWARD], c.r1.at[j, DOWNWARD], c.sum_minus)

    def sum_second(c, j):
        arrived(c, (FIRST, j), c.r1.at[j])
        if j in ASIDE:
            for d in range(4):
                at = piece(c.q(d, 0))
                c.p[j, at] = c.p[j, at] + decode(c.r1[j, d // 2, (first, second)[d % 2]])
            at = piece(c.q(2, 0))
            c.s2[j, UPWARD, :, lo] = encode(c.p[j, at, lo])
            c.s2[j, DOWNWARD, :, hi] = encode(c.p[j, at, hi])
            send(c, (SECOND, j), c.s2.at[j, UPWARD, :, lo], c.r2.at[j, UPWARD, :, lo], c.sum_plus)
            send(c, (SECOND, j), c.s2.at[j, DOWNWARD, :, hi], c.r2.at[j, DOWNWARD, :, hi], c.sum_minus)
            return
        c.s2[j, UPWARD] = encode(c.p[j, piece(c.q(1, 0))] + decode(c.r1[j, UPWARD, first]))
        send(c, (SECOND, j), c.s2.at[j, UPWARD], c.r2.at[j, UPWARD], c.sum_plus)
        c.s2[j, DOWNWARD] = encode(c.p[j, piece(c.q(3, 1))] + decode(c.r1[j, DOWNWARD, first]))
        send(c, (SECOND, j), c.s2.at[j, DOWNWARD], c.r2.at[j, DOWNWARD], c.sum_minus)

    def sum_partner(c, j):
        if j in ASIDE:
            arrived(c, (SECOND, j), c.r2.at[j, UPWARD])
            k = ASIDE.index(j)
            up, down = piece(c.q(1, 0)), piece(c.q(3, 0))
            c.s4[k, UPWARD, :, lo] = encode(c.p[j, up, lo] + decode(c.r2[j, UPWARD, :, lo]))
            c.s4[k, UPWARD, :, hi] = encode(c.p[j, up, hi])
            send(c, (THIRD, j), c.s4.at[k, UPWARD], c.r4.at[k, UPWARD], c.sum_plus)
            c.s4[k, DOWNWARD, :, lo] = encode(c.p[j, down, lo])
            c.s4[k, DOWNWARD, :, hi] = encode(c.p[j, down, hi] + decode(c.r2[j, DOWNWARD, :, hi]))
            send(c, (THIRD, j), c.s4.at[k, DOWNWARD], c.r4.at[k, DOWNWARD], c.sum_minus)
            return
        arrived(c, (SECOND, j), c.r2.at[j])
        c.s3[j] = encode(c.p[j, piece(c.q(0, 1))] + decode(c.r1[j, UPWARD, second]) + decode(c.r2[j, DOWNWARD]))
        send(c, (THIRD, j), c.s3.at[j], c.r3.at[j], c.sum_partner)
        at = piece(c.q(0, 0))
        c.p[j, at] = c.p[j, at] + decode(c.r1[j, DOWNWARD, second]) + decode(c.r2[j, UPWARD])

    def finish(c, j):
        at = piece(c.q(0, 0))
        if j in ASIDE:
            k = ASIDE.index(j)
            arrived(c, (THIRD, j), c.r4.at[k])
            c.rot[j, at] = (c.p[j, at] + decode(c.r4[k, UPWARD]) + decode(c.r4[k, DOWNWARD])).astype(BF16)
        else:
            arrived(c, (THIRD, j), c.r3.at[j])
            c.rot[j, at] = (c.p[j, at] + decode(c.r3[j])).astype(BF16)
        ref = c.rot.at[j, at]
        if j in DIRECT:
            send(c, (DONE, SIDE, j), ref, ref, c.sum_partner)
            for to in (c.sum_plus, c.sum_minus, c.sum_two):
                send(c, (DONE, j), ref, ref, to)
        else:
            send(c, (DONE, j), ref, ref, c.sum_plus)
            send(c, (DONE, j), ref, ref, c.sum_minus)
            send(c, (DONE, SIDE, j), ref, ref, c.sum_partner)

    def spread(c, j):
        arrived(c, (DONE, j), c.rot.at[j, pl.ds(0, 2 * PIECE)])
        ref = c.rot.at[j, piece(c.q(3, 0)), lo]
        send(c, (HALVES, j), ref, ref, c.sum_plus)
        ref = c.rot.at[j, piece(c.q(1, 0)), hi]
        send(c, (HALVES, j), ref, ref, c.sum_minus)
        if j in LATER:
            for d in (3, 1):
                ref = c.rot.at[j, piece(c.q(d, 0))]
                send(c, (DONE, SIDE, j), ref, ref, c.sum_partner)

    def across(c, j):
        if j in LATER:
            arrived(c, (HALVES, j), c.rot.at[j, first])
            ref = c.rot.at[j, piece(c.q(2, 0))]
            send(c, (DONE, SIDE, j), ref, ref, c.sum_partner)
            return
        arrived(c, (DONE, SIDE, j), c.rot.at[j, first])
        ref = c.rot.at[j, piece(c.q(0, 1))]
        if j in DIRECT:
            for to in (c.sum_two, c.sum_plus, c.sum_minus):
                send(c, (HALVES, j), ref, ref, to)
        else:
            send(c, (ACROSS, j), ref, ref, c.sum_plus)
            send(c, (ACROSS, j), ref, ref, c.sum_minus)

    def spread_across(c, j):
        arrived(c, (ACROSS, j), c.rot.at[j, pl.ds(0, 2 * PIECE)])
        ref = c.rot.at[j, piece(c.q(3, 1)), lo]
        send(c, (HALVES, j), ref, ref, c.sum_plus)
        ref = c.rot.at[j, piece(c.q(1, 1)), hi]
        send(c, (HALVES, j), ref, ref, c.sum_minus)

    def share_rows(c, j, rows):
        now = sum(j > upto for _, upto in PASSES)
        if c is a:
            send(g, (SHARED, now), rot_a.at[j, rows], rot_ao.at[j, rows], other)
        else:
            send(g, (SHARED, now), rot_g.at[j, rows, hi], rot_go.at[j, rows], other)

    def share_early(c, j):
        arrived(c, (DONE, j), c.rot.at[j, pl.ds(0, 3 * PIECE)])
        for d in range(4):
            share_rows(c, j, piece(c.q(d, 0)))

    def share(c, j):
        if j in DIRECT:
            arrived(c, (HALVES, j), c.rot.at[j, pl.ds(0, 3 * PIECE)])
            for d in range(4):
                share_rows(c, j, piece(c.q(d, 1)))
            return
        if j in LATER:
            arrived(c, (DONE, SIDE, j), c.rot.at[j, pl.ds(0, 4 * PIECE)])
        else:
            arrived(c, (HALVES, j), c.rot.at[j, pl.ds(0, 2 * PIECE)])
        share_rows(c, j, pl.ds(0, HALF))

    def receive(now):
        above, upto = (PASSES + ((SLOTS - 2, SLOTS - 1),))[now]
        arrived(g, (SHARED, now), wa.at[pl.ds(0, (upto - above) * (HALF + HALF // 2))])

    def ring_slot(up):
        return up + (up // 2) * (1 - 2 * (up % 2))

    def a_slot(t):
        return ring_slot((t % 4 + 4 - x) % 4) + 4 * ((t // 4 + yh) % 2)

    def g_slot(t):
        return ring_slot((t // 2 + 4 - z) % 4) + 4 * ((t + yl) % 2)

    def correlate(above, upto):
        @pl.loop(0, SLOTS)
        def _(t):
            last = jnp.maximum(a_slot(t), g_slot(t))

            @pl.when((last > above) & (last <= upto))
            def _():
                rows = jnp.concatenate([rot_g[g_slot(t), :, lo], rot_go[g_slot(t)]], axis=0)
                columns = jnp.concatenate([rot_a[a_slot(t)], rot_ao[a_slot(t)]], axis=0)
                sums[t // 4] += lax.dot_general(
                    rows, columns, (((0,), (0,)), ((), ())), preferred_element_type=F32)

    steps = (own, forward_up, forward_down, partner_lo, partner_hi, partner_forward_up, partner_forward_down,
             multiply, sum_second, sum_partner, finish, spread, across, spread_across, share, None, share_early)
    for code in ORDER:
        c, step, j = (g, a)[code // 1000], code % 1000 // 10, code % 10
        if step < 7:
            steps[step](c)
        elif step < len(steps):
            steps[step](c, j)
        else:
            receive(j)
            correlate(*PASSES[j])

    receive(len(PASSES))
    last_a = (yh + 1) % 2 * 4 + (x + 2) % 4
    last_g = (z + 2) % 4 * 2 + (yl + 1) % 2
    distinct = jnp.where(last_a == last_g, 0.0, 1.0)
    in_first_a = jnp.where(last_a < 4, 1.0, 0.0)
    in_first_g = jnp.where(last_g < 4, distinct, 0.0)

    @pl.loop(0, WIDE // LAST_TILE)
    def _(n):
        cols = pl.ds(pl.multiple_of(n * LAST_TILE, LAST_TILE), LAST_TILE)

        def product(t):
            rows = jnp.concatenate([rot_g[g_slot(t), :, lo], rot_go[g_slot(t)]], axis=0)
            columns = jnp.concatenate([rot_a[a_slot(t), :, cols], rot_ao[a_slot(t), :, cols]], axis=0)
            return lax.dot_general(rows, columns, (((0,), (0,)), ((), ())), preferred_element_type=F32)

        for_a, for_g = product(last_a), product(last_g)
        block0 = sums[0, :, cols] + for_a * in_first_a + for_g * in_first_g
        block1 = sums[1, :, cols] + for_a * (1.0 - in_first_a) + for_g * (distinct - in_first_g)
        out[:, cols] = (block0 * block0 + block1 * block1) * (1.0 / TOKENS)

    assert len(names) == ARRIVALS
    pltpu.make_async_copy(total, total, send_sem).wait()


def on_device(acts, grads, qa, qs):
    vm = pltpu.VMEM
    sums = [vm((SLOTS, 2, 2 * PIECE, WIDE), BF16)] * 2 + [vm((SLOTS, 2, PIECE, WIDE), BF16)] * 2
    sums += [vm((SLOTS, PIECE, WIDE), BF16)] * 2 + [vm((max(len(ASIDE), 1), 2, PIECE, WIDE), BF16)] * 2
    args = [pltpu.with_memory_space_constraint(v, pltpu.HBM) for v in (acts, grads, qa, qs)]
    correction, _ = pl.pallas_call(
        kernel,
        out_shape=(jax.ShapeDtypeStruct((NARROW, WIDE), F32), pltpu.HBM((SENT, WIDE), BF16)),
        in_specs=[pl.BlockSpec(memory_space=pl.ANY)] * 4,
        out_specs=(pl.BlockSpec(memory_space=pltpu.VMEM), pl.BlockSpec(memory_space=pltpu.HBM)),
        scratch_shapes=[
            vm((SEQS, NARROW, WIDE), F32),
            vm((SLOTS, HALF, WIDE), BF16), vm((SLOTS, HALF, WIDE), BF16),
            vm((WIDE, WIDE), BF16), vm((WIDE, WIDE), BF16),
            vm((SLOTS, HALF, WIDE), F32), vm((SLOTS, HALF, WIDE), F32),
            vm((SLOTS, HALF, WIDE), BF16), vm((SLOTS, HALF, WIDE), BF16),
            vm((SLOTS, HALF, WIDE), BF16), vm((SLOTS, HALF, NARROW), BF16),
            *sums, *sums,
            pltpu.SemaphoreType.DMA((4,)),
            pltpu.SemaphoreType.DMA, pltpu.SemaphoreType.DMA((ARRIVALS,)),
        ],
        compiler_params=pltpu.CompilerParams(
            collective_id=0, has_side_effects=True, vmem_limit_bytes=48 * 2 ** 20),
        cost_estimate=pl.CostEstimate(flops=6442450944, bytes_accessed=5 * 2 ** 20, transcendentals=0),
        name="rotate_and_correlate",
    )(*args)
    return correction


def solution(mesh):
    return jax.shard_map(
        on_device,
        mesh=mesh,
        in_specs=(P("row", "col"), P("col", "row"), P("col", "row"), P("row", "col")),
        out_specs=P("col", "row"),
        check_vma=False,
    )
```

```python
import jax
import jax.numpy as jnp
from jax import lax
from jax.experimental import pallas as pl
from jax.experimental.pallas import tpu as pltpu
from jax.sharding import PartitionSpec as P

MESH = pl.DeviceIdType.MESH
F32, BF16 = jnp.float32, jnp.bfloat16

TOKENS, D, SEQS = 2048, 8192, 2
SLOTS = 8
HALF = TOKENS // SLOTS // 2
PIECE = HALF // SLOTS
WIDE = 1024
NARROW = WIDE // 2
TILE = 512
LAST_TILE = 512
DIRECT = (6, 7)
ASIDE = (0, 3)
LATER = (3,)
ARRIVALS = 139
SENT = 8000

PASSES = ((-1, 0), (0, 1), (1, 2), (2, 4), (4, 6))

UP = 2.0 ** 30

ORDER = (
    0, 1000, 1070, 30, 1020, 10, 20, 1010, 71, 1072, 40, 74, 70, 1030, 72, 1073, 1071, 1082, 1040, 1074, 60, 84, 50,
    81, 73, 1081, 82, 80, 75, 76, 1092, 1084, 1080, 1060, 1075, 94, 91, 92, 1083, 1050, 1076, 1091, 1094, 83, 85,
    1090, 90, 1102, 77, 104, 1085, 86, 101, 1093, 1101, 1086, 1104, 1100, 1077, 95, 93, 102, 1095, 1103, 100, 1096,
    1122, 124, 1121, 1120, 96, 114, 87, 121, 103, 1087, 1105, 105, 1112, 1113, 1110, 122, 134, 120, 111, 97, 1124,
    1106, 1130, 1097, 1111, 106, 131, 1114, 1125, 113, 125, 1123, 1131, 1132, 130, 110, 1134, 115, 1126, 132, 112,
    1115, 107, 1107, 123, 144, 135, 126, 1141, 1135, 1142, 1140, 140, 141, 1143, 1144, 142, 1127, 127, 1166, 1146,
    170, 143, 171, 145, 172, 1145, 166, 146, 1167, 167, 173, 1147, 147, 174,
)


def encode(v):
    v = v * UP
    return (v * v * v).astype(BF16)


def decode(c):
    c = c.astype(F32)
    size = jnp.maximum(jnp.abs(c), 2.0 ** -126)
    return c * (jnp.exp2(jnp.log2(size) * (-2.0 / 3.0)) * (1.0 / UP))


class Chain:
    def __init__(self, **refs):
        self.__dict__.update(refs)


def kernel(acts, grads, qa, qs, out, total,
           sums, xa, xg, wa, wg, pa, pg, rot_a, rot_g, rot_ao, rot_go,
           s1a, r1a, s2a, r2a, s3a, r3a, s4a, r4a, s1g, r1g, s2g, r2g, s3g, r3g, s4g, r4g,
           local_sem, send_sem, recv_sem):
    row, col = lax.axis_index("row"), lax.axis_index("col")
    yh, x = row // 4, row % 4
    z, yl, h = col // 4, (col // 2) % 2, col % 2

    def dev(dyh, dx, dz, dyl, core):
        return ((yh + dyh) % 2 * 4 + (x + dx) % 4, (z + dz) % 4 * 4 + (yl + dyl) % 2 * 2 + core)

    x_plus, x_minus = dev(0, 1, 0, 0, h), dev(0, 3, 0, 0, h)
    z_plus, z_minus = dev(0, 0, 1, 0, h), dev(0, 0, 3, 0, h)
    y_far, y_near = dev(1, 0, 0, 0, h), dev(0, 0, 0, 1, h)
    other = dev(0, 0, 0, 0, 1 - h)
    x_plus_o, x_minus_o, y_far_o = dev(0, 1, 0, 0, 1 - h), dev(0, 3, 0, 0, 1 - h), dev(1, 0, 0, 0, 1 - h)

    barrier = pltpu.get_barrier_semaphore()
    x_two, z_two = dev(0, 2, 0, 0, h), dev(0, 0, 2, 0, h)
    neighbours = (x_plus, x_minus, z_plus, z_minus, y_far, y_near, other, x_plus_o, x_minus_o, y_far_o, x_two, z_two)
    for n in neighbours:
        pl.semaphore_signal(barrier, inc=1, device_id=n, device_id_type=MESH)

    names = {}

    def arrival(c, name):
        return recv_sem.at[names.setdefault((c.at,) + name, len(names))]

    def send(c, name, src, dst, to):
        pltpu.make_async_remote_copy(
            src_ref=src, dst_ref=dst, send_sem=send_sem, recv_sem=arrival(c, name),
            device_id=to, device_id_type=MESH).start()

    def arrived(c, name, ref):
        pltpu.make_async_remote_copy(
            src_ref=ref, dst_ref=ref, send_sem=send_sem, recv_sem=arrival(c, name),
            device_id=other, device_id_type=MESH).wait_recv()

    def piece(q):
        return pl.ds(pl.multiple_of(q * PIECE, PIECE), PIECE)

    lo, hi = pl.ds(0, NARROW), pl.ds(NARROW, NARROW)
    mine = pl.ds(pl.multiple_of(h * HALF, HALF), HALF)
    its = pl.ds(pl.multiple_of((1 - h) * HALF, HALF), HALF)
    first, second = pl.ds(0, PIECE), pl.ds(PIECE, PIECE)

    a = Chain(at=1, plus=x_plus, minus=x_minus, partner=y_far,
              sum_plus=z_plus, sum_minus=z_minus, sum_two=z_two, sum_partner=y_near,
              plus_o=x_plus_o, minus_o=x_minus_o, partner_o=y_far_o,
              own_lo=acts.at[mine], own_hi=acts.at[its],
              q=lambda d, e: ((z + d) % 4) * 2 + (yl + e) % 2,
              x=xa, w=wa, p=pa, rot=rot_a, s1=s1a, r1=r1a, s2=s2a, r2=r2a, s3=s3a, r3=r3a,
              s4=s4a, r4=r4a)
    g = Chain(at=0, plus=z_plus, minus=z_minus, partner=y_near,
              sum_plus=x_plus, sum_minus=x_minus, sum_two=x_two, sum_partner=y_far,
              plus_o=z_plus, minus_o=z_minus, partner_o=y_near,
              own_lo=grads.at[:, lo], own_hi=grads.at[:, hi],
              q=lambda d, e: ((yh + e) % 2) * 4 + (x + d) % 4,
              x=xg, w=wg, p=pg, rot=rot_g, s1=s1g, r1=r1g, s2=s2g, r2=r2g, s3=s3g, r3=r3g,
              s4=s4g, r4=r4g)

    local = [
        pltpu.make_async_copy(grads, xg.at[0], local_sem.at[0]),
        pltpu.make_async_copy(acts.at[mine], xa.at[0, :, lo], local_sem.at[1]),
        pltpu.make_async_copy(qs, wg.at[:, lo], local_sem.at[2]),
        pltpu.make_async_copy(qa, wa.at[lo], local_sem.at[3]),
    ]
    for copy in local:
        copy.start()

    pl.semaphore_wait(barrier, len(neighbours))

    UPWARD, DOWNWARD, SIDE = 0, 1, 2
    OWN, AHEAD, PARTNER, PARTNER_AHEAD, SWAP, BASIS, FIRST, SECOND, THIRD, DONE, ACROSS, HALVES, SHARED = range(13)

    def own(c):
        send(c, (OWN, UPWARD, 0), c.own_lo, c.x.at[2, :, lo], c.plus)
        send(c, (OWN, DOWNWARD, 1), c.own_hi, c.x.at[1, :, hi], c.minus_o)
        send(c, (OWN, SIDE, 0), c.own_lo, c.x.at[4, :, lo], c.partner)
        send(c, (OWN, UPWARD, 1), c.own_hi, c.x.at[2, :, hi], c.plus_o)
        send(c, (OWN, DOWNWARD, 0), c.own_lo, c.x.at[1, :, lo], c.minus)
        send(c, (OWN, SIDE, 1), c.own_hi, c.x.at[4, :, hi], c.partner_o)
        if c is a:
            send(c, (SWAP,), acts.at[its], xa.at[0, :, hi], other)
            send(c, (BASIS,), qa, wa.at[hi], other)
            sums[...] = jnp.zeros_like(sums)
        else:
            send(c, (BASIS,), qs, wg.at[:, hi], other)

    def forward_up(c):
        arrived(c, (OWN, UPWARD, 0), c.x.at[2, :, lo])
        send(c, (AHEAD,), c.x.at[2, :, lo], c.x.at[3, :, lo], c.plus)

    def forward_down(c):
        arrived(c, (OWN, DOWNWARD, 1), c.x.at[1, :, hi])
        send(c, (AHEAD,), c.x.at[1, :, hi], c.x.at[3, :, hi], c.minus)

    def partner_lo(c):
        arrived(c, (OWN, SIDE, 0), c.x.at[4, :, lo])
        send(c, (PARTNER, UPWARD, 0), c.x.at[4, :, lo], c.x.at[6, :, lo], c.plus)
        send(c, (PARTNER, DOWNWARD, 0), c.x.at[4, :, lo], c.x.at[5, :, lo], c.minus)

    def partner_hi(c):
        arrived(c, (OWN, SIDE, 1), c.x.at[4, :, hi])
        send(c, (PARTNER, DOWNWARD, 1), c.x.at[4, :, hi], c.x.at[5, :, hi], c.minus)
        send(c, (PARTNER, UPWARD, 1), c.x.at[4, :, hi], c.x.at[6, :, hi], c.plus)

    def partner_forward_up(c):
        arrived(c, (PARTNER, UPWARD, 0), c.x.at[6, :, lo])
        send(c, (PARTNER_AHEAD,), c.x.at[6, :, lo], c.x.at[7, :, lo], c.plus)

    def partner_forward_down(c):
        arrived(c, (PARTNER, DOWNWARD, 1), c.x.at[5, :, hi])
        send(c, (PARTNER_AHEAD,), c.x.at[5, :, hi], c.x.at[7, :, hi], c.minus)

    needs = {1: ((OWN, DOWNWARD, 0), lo), 2: ((OWN, UPWARD, 1), hi), 3: ((AHEAD,), None),
             5: ((PARTNER, DOWNWARD, 0), lo), 6: ((PARTNER, UPWARD, 1), hi), 7: ((PARTNER_AHEAD,), None)}
    begun = set()

    def multiply(c, j):
        if c.at not in begun:
            begun.add(c.at)
            for copy in (local[0], local[2]) if c is g else (local[1], local[3]):
                copy.wait()
            arrived(c, (BASIS,), c.w.at[hi])
        if j == 0 and c is a:
            arrived(c, (SWAP,), c.x.at[0, :, hi])
        if j in needs:
            name, cols = needs[j]
            arrived(c, name, c.x.at[j] if cols is None else c.x.at[j, :, cols])

        @pl.loop(0, WIDE // TILE)
        def _(n):
            cols = pl.ds(pl.multiple_of(n * TILE, TILE), TILE)
            c.p[j, :, cols] = jnp.dot(c.x[j], c.w[:, cols], preferred_element_type=F32)

        if j in ASIDE:
            for d in range(4):
                c.s1[j, d // 2, (first, second)[d % 2]] = encode(c.p[j, piece(c.q(d, 1))])
            send(c, (FIRST, j), c.s1.at[j], c.r1.at[j], c.sum_partner)
            return
        c.s1[j, UPWARD, first] = encode(c.p[j, piece(c.q(2, 0))])
        c.s1[j, UPWARD, second] = encode(c.p[j, piece(c.q(1, 1))])
        send(c, (FIRST, j), c.s1.at[j, UPWARD], c.r1.at[j, UPWARD], c.sum_plus)
        c.s1[j, DOWNWARD, first] = encode(c.p[j, piece(c.q(2, 1))])
        c.s1[j, DOWNWARD, second] = encode(c.p[j, piece(c.q(3, 0))])
        send(c, (FIRST, j), c.s1.at[j, DOWNWARD], c.r1.at[j, DOWNWARD], c.sum_minus)

    def sum_second(c, j):
        arrived(c, (FIRST, j), c.r1.at[j])
        if j in ASIDE:
            for d in range(4):
                at = piece(c.q(d, 0))
                c.p[j, at] = c.p[j, at] + decode(c.r1[j, d // 2, (first, second)[d % 2]])
            at = piece(c.q(2, 0))
            c.s2[j, UPWARD, :, lo] = encode(c.p[j, at, lo])
            c.s2[j, DOWNWARD, :, hi] = encode(c.p[j, at, hi])
            send(c, (SECOND, j), c.s2.at[j, UPWARD, :, lo], c.r2.at[j, UPWARD, :, lo], c.sum_plus)
            send(c, (SECOND, j), c.s2.at[j, DOWNWARD, :, hi], c.r2.at[j, DOWNWARD, :, hi], c.sum_minus)
            return
        c.s2[j, UPWARD] = encode(c.p[j, piece(c.q(1, 0))] + decode(c.r1[j, UPWARD, first]))
        send(c, (SECOND, j), c.s2.at[j, UPWARD], c.r2.at[j, UPWARD], c.sum_plus)
        c.s2[j, DOWNWARD] = encode(c.p[j, piece(c.q(3, 1))] + decode(c.r1[j, DOWNWARD, first]))
        send(c, (SECOND, j), c.s2.at[j, DOWNWARD], c.r2.at[j, DOWNWARD], c.sum_minus)

    def sum_partner(c, j):
        if j in ASIDE:
            arrived(c, (SECOND, j), c.r2.at[j, UPWARD])
            k = ASIDE.index(j)
            up, down = piece(c.q(1, 0)), piece(c.q(3, 0))
            c.s4[k, UPWARD, :, lo] = encode(c.p[j, up, lo] + decode(c.r2[j, UPWARD, :, lo]))
            c.s4[k, UPWARD, :, hi] = encode(c.p[j, up, hi])
            send(c, (THIRD, j), c.s4.at[k, UPWARD], c.r4.at[k, UPWARD], c.sum_plus)
            c.s4[k, DOWNWARD, :, lo] = encode(c.p[j, down, lo])
            c.s4[k, DOWNWARD, :, hi] = encode(c.p[j, down, hi] + decode(c.r2[j, DOWNWARD, :, hi]))
            send(c, (THIRD, j), c.s4.at[k, DOWNWARD], c.r4.at[k, DOWNWARD], c.sum_minus)
            return
        arrived(c, (SECOND, j), c.r2.at[j])
        c.s3[j] = encode(c.p[j, piece(c.q(0, 1))] + decode(c.r1[j, UPWARD, second]) + decode(c.r2[j, DOWNWARD]))
        send(c, (THIRD, j), c.s3.at[j], c.r3.at[j], c.sum_partner)
        at = piece(c.q(0, 0))
        c.p[j, at] = c.p[j, at] + decode(c.r1[j, DOWNWARD, second]) + decode(c.r2[j, UPWARD])

    def finish(c, j):
        at = piece(c.q(0, 0))
        if j in ASIDE:
            k = ASIDE.index(j)
            arrived(c, (THIRD, j), c.r4.at[k])
            c.rot[j, at] = (c.p[j, at] + decode(c.r4[k, UPWARD]) + decode(c.r4[k, DOWNWARD])).astype(BF16)
        else:
            arrived(c, (THIRD, j), c.r3.at[j])
            c.rot[j, at] = (c.p[j, at] + decode(c.r3[j])).astype(BF16)
        ref = c.rot.at[j, at]
        if j in DIRECT:
            send(c, (DONE, SIDE, j), ref, ref, c.sum_partner)
            for to in (c.sum_plus, c.sum_minus, c.sum_two):
                send(c, (DONE, j), ref, ref, to)
        else:
            send(c, (DONE, j), ref, ref, c.sum_plus)
            send(c, (DONE, j), ref, ref, c.sum_minus)
            send(c, (DONE, SIDE, j), ref, ref, c.sum_partner)

    def spread(c, j):
        arrived(c, (DONE, j), c.rot.at[j, pl.ds(0, 2 * PIECE)])
        ref = c.rot.at[j, piece(c.q(3, 0)), lo]
        send(c, (HALVES, j), ref, ref, c.sum_plus)
        ref = c.rot.at[j, piece(c.q(1, 0)), hi]
        send(c, (HALVES, j), ref, ref, c.sum_minus)
        if j in LATER:
            for d in (3, 1):
                ref = c.rot.at[j, piece(c.q(d, 0))]
                send(c, (DONE, SIDE, j), ref, ref, c.sum_partner)

    def across(c, j):
        if j in LATER:
            arrived(c, (HALVES, j), c.rot.at[j, first])
            ref = c.rot.at[j, piece(c.q(2, 0))]
            send(c, (DONE, SIDE, j), ref, ref, c.sum_partner)
            return
        arrived(c, (DONE, SIDE, j), c.rot.at[j, first])
        ref = c.rot.at[j, piece(c.q(0, 1))]
        if j in DIRECT:
            for to in (c.sum_two, c.sum_plus, c.sum_minus):
                send(c, (HALVES, j), ref, ref, to)
        else:
            send(c, (ACROSS, j), ref, ref, c.sum_plus)
            send(c, (ACROSS, j), ref, ref, c.sum_minus)

    def spread_across(c, j):
        arrived(c, (ACROSS, j), c.rot.at[j, pl.ds(0, 2 * PIECE)])
        ref = c.rot.at[j, piece(c.q(3, 1)), lo]
        send(c, (HALVES, j), ref, ref, c.sum_plus)
        ref = c.rot.at[j, piece(c.q(1, 1)), hi]
        send(c, (HALVES, j), ref, ref, c.sum_minus)

    def share_rows(c, j, rows):
        now = sum(j > upto for _, upto in PASSES)
        if c is a:
            send(g, (SHARED, now), rot_a.at[j, rows], rot_ao.at[j, rows], other)
        else:
            send(g, (SHARED, now), rot_g.at[j, rows, hi], rot_go.at[j, rows], other)

    def share_early(c, j):
        arrived(c, (DONE, j), c.rot.at[j, pl.ds(0, 3 * PIECE)])
        for d in range(4):
            share_rows(c, j, piece(c.q(d, 0)))

    def share(c, j):
        if j in DIRECT:
            arrived(c, (HALVES, j), c.rot.at[j, pl.ds(0, 3 * PIECE)])
            for d in range(4):
                share_rows(c, j, piece(c.q(d, 1)))
            return
        if j in LATER:
            arrived(c, (DONE, SIDE, j), c.rot.at[j, pl.ds(0, 4 * PIECE)])
        else:
            arrived(c, (HALVES, j), c.rot.at[j, pl.ds(0, 2 * PIECE)])
        share_rows(c, j, pl.ds(0, HALF))

    def receive(now):
        above, upto = (PASSES + ((SLOTS - 2, SLOTS - 1),))[now]
        arrived(g, (SHARED, now), wa.at[pl.ds(0, (upto - above) * (HALF + HALF // 2))])

    def ring_slot(up):
        return up + (up // 2) * (1 - 2 * (up % 2))

    def a_slot(t):
        return ring_slot((t % 4 + 4 - x) % 4) + 4 * ((t // 4 + yh) % 2)

    def g_slot(t):
        return ring_slot((t // 2 + 4 - z) % 4) + 4 * ((t + yl) % 2)

    def correlate(above, upto):
        @pl.loop(0, SLOTS)
        def _(t):
            last = jnp.maximum(a_slot(t), g_slot(t))

            @pl.when((last > above) & (last <= upto))
            def _():
                rows = jnp.concatenate([rot_g[g_slot(t), :, lo], rot_go[g_slot(t)]], axis=0)
                columns = jnp.concatenate([rot_a[a_slot(t)], rot_ao[a_slot(t)]], axis=0)
                sums[t // 4] += lax.dot_general(
                    rows, columns, (((0,), (0,)), ((), ())), preferred_element_type=F32)

    steps = (own, forward_up, forward_down, partner_lo, partner_hi, partner_forward_up, partner_forward_down,
             multiply, sum_second, sum_partner, finish, spread, across, spread_across, share, None, share_early)
    for code in ORDER:
        c, step, j = (g, a)[code // 1000], code % 1000 // 10, code % 10
        if step < 7:
            steps[step](c)
        elif step < len(steps):
            steps[step](c, j)
        else:
            receive(j)
            correlate(*PASSES[j])

    receive(len(PASSES))
    last_a = (yh + 1) % 2 * 4 + (x + 2) % 4
    last_g = (z + 2) % 4 * 2 + (yl + 1) % 2
    distinct = jnp.where(last_a == last_g, 0.0, 1.0)
    in_first_a = jnp.where(last_a < 4, 1.0, 0.0)
    in_first_g = jnp.where(last_g < 4, distinct, 0.0)

    @pl.loop(0, WIDE // LAST_TILE)
    def _(n):
        cols = pl.ds(pl.multiple_of(n * LAST_TILE, LAST_TILE), LAST_TILE)

        def product(t):
            rows = jnp.concatenate([rot_g[g_slot(t), :, lo], rot_go[g_slot(t)]], axis=0)
            columns = jnp.concatenate([rot_a[a_slot(t), :, cols], rot_ao[a_slot(t), :, cols]], axis=0)
            return lax.dot_general(rows, columns, (((0,), (0,)), ((), ())), preferred_element_type=F32)

        for_a, for_g = product(last_a), product(last_g)
        block0 = sums[0, :, cols] + for_a * in_first_a + for_g * in_first_g
        block1 = sums[1, :, cols] + for_a * (1.0 - in_first_a) + for_g * (distinct - in_first_g)
        out[:, cols] = (block0 * block0 + block1 * block1) * (1.0 / TOKENS)

    assert len(names) == ARRIVALS
    pltpu.make_async_copy(total, total, send_sem).wait()


def on_device(acts, grads, qa, qs):
    vm = pltpu.VMEM
    sums = [vm((SLOTS, 2, 2 * PIECE, WIDE), BF16)] * 2 + [vm((SLOTS, 2, PIECE, WIDE), BF16)] * 2
    sums += [vm((SLOTS, PIECE, WIDE), BF16)] * 2 + [vm((max(len(ASIDE), 1), 2, PIECE, WIDE), BF16)] * 2
    args = [pltpu.with_memory_space_constraint(v, pltpu.HBM) for v in (acts, grads, qa, qs)]
    correction, _ = pl.pallas_call(
        kernel,
        out_shape=(jax.ShapeDtypeStruct((NARROW, WIDE), F32), pltpu.HBM((SENT, WIDE), BF16)),
        in_specs=[pl.BlockSpec(memory_space=pl.ANY)] * 4,
        out_specs=(pl.BlockSpec(memory_space=pltpu.VMEM), pl.BlockSpec(memory_space=pltpu.HBM)),
        scratch_shapes=[
            vm((SEQS, NARROW, WIDE), F32),
            vm((SLOTS, HALF, WIDE), BF16), vm((SLOTS, HALF, WIDE), BF16),
            vm((WIDE, WIDE), BF16), vm((WIDE, WIDE), BF16),
            vm((SLOTS, HALF, WIDE), F32), vm((SLOTS, HALF, WIDE), F32),
            vm((SLOTS, HALF, WIDE), BF16), vm((SLOTS, HALF, WIDE), BF16),
            vm((SLOTS, HALF, WIDE), BF16), vm((SLOTS, HALF, NARROW), BF16),
            *sums, *sums,
            pltpu.SemaphoreType.DMA((4,)),
            pltpu.SemaphoreType.DMA, pltpu.SemaphoreType.DMA((ARRIVALS,)),
        ],
        compiler_params=pltpu.CompilerParams(
            collective_id=0, has_side_effects=True, vmem_limit_bytes=48 * 2 ** 20),
        cost_estimate=pl.CostEstimate(flops=6442450944, bytes_accessed=5 * 2 ** 20, transcendentals=0),
        name="rotate_and_correlate",
    )(*args)
    return correction


def solution(mesh):
    return jax.shard_map(
        on_device,
        mesh=mesh,
        in_specs=(P("row", "col"), P("col", "row"), P("col", "row"), P("row", "col")),
        out_specs=P("col", "row"),
        check_vma=False,
    )
```
